32 devices in a mesh: box: 4 (over z), dir: 8 (over y, x, core).
Axes of the slice: x: 2, y: 2, z: 4, core: 2. Of those that a mesh axis runs over, the one named last changes fastest.
Arguments:
- leaf_out: bfloat16 [2, 2048, 1024], P(None, ('box', 'dir')), may hold values from -6 to 6
- interp_mid: bfloat16 [1024, 4096], replicated, may hold values from -0.1875 to 0.1875
- shift_mid: float32 [8, 4096], replicated, may hold values from -3.140625 to 3.140625
- trans_mid: float32 [2, 316, 4096], P(None, None, 'dir'), may hold values from -0.5 to 0.5
- list_mid: int32 [256, 64], replicated, may hold values from 0 to 255
- offset_mid: int32 [256, 64], replicated, may hold values from 0 to 315
- interp_top: bfloat16 [8, 512, 2048], P('dir'), may hold values from -0.25 to 0.25
- shift_top: float32 [8, 8, 2048], P(None, 'dir'), may hold values from -3.140625 to 3.140625
- trans_top: float32 [2, 316, 8, 2048], P(None, None, 'dir', 'box'), may hold values from -0.5 to 0.5
- list_top: int32 [32, 64], replicated, may hold values from 0 to 31
- offset_top: int32 [32, 64], replicated, may hold values from 0 to 315
Outputs:
- leaf_in: float32 [2, 2048, 1024], P(None, ('box', 'dir'))
The draws below stay inside these ranges and needn't reach their ends.
Inputs may be any that keep to these rules, and one draw needn't show every extreme that they name: `list_mid`: middle box indices. `offset_mid`: offset indices. `list_top`: top box indices. `offset_top`: offset indices.
All inputs are finite; a program needn't handle non-finite values.
Results may differ from the reference program's by a relative error of at most 0.014.
Values may be sent and summed in bfloat16 or wider, within the bound.
No kernel may reach another device: no remote copies, remote signals or barrier semaphores. Data moves between devices by JAX's collectives and lax.ppermute only.
A program may use at most 64 MiB of HBM per device.

```python
import math
import jax
import jax.numpy as jnp
from jax import lax

K0 = 1024
K1 = 4096
K2 = 16384
NLIST = 64
NOFF = 316
LEAF_DEV = 64
LEAVES = 2048
MID_BOXES = 256
TOP_BOXES = 32
SECT = 8
K1_SECT = 512
K2_SECT = 2048


def with_ends(values, stream_key, least, top_value):
    longest = values.shape.index(max(values.shape))
    spots = []
    for shift in (0, 1):
        where = [jax.random.randint(jax.random.fold_in(stream_key, axis), (), 0, length) for axis, length in enumerate(values.shape)]
        where[longest] = (where[longest] + shift) % values.shape[longest]
        spots.append(tuple(where))
    return values.at[spots[0]].set(least).at[spots[1]].set(top_value)


def block_scale(key, shape, pieces, least, top_value):
    def one(axis_at, shards_of):
        steps = jax.random.uniform(jax.random.fold_in(jax.random.fold_in(key, 6), axis_at), (shards_of,), jnp.float32, least / len(pieces), top_value / len(pieces))
        return jnp.repeat(jnp.exp(steps), shape[axis_at] // shards_of).reshape((-1,) + (1,) * (len(shape) - axis_at - 1))

    factor_of = one(*pieces[0])
    for cut in pieces[1:]:
        factor_of = factor_of * one(*cut)
    return factor_of


def scatter_about(stream_key, shape, width, most, pieces=(), dtype=jnp.bfloat16):
    result = width * jax.random.normal(stream_key, shape, jnp.float32)
    if pieces:
        result = result * block_scale(stream_key, shape, pieces, -0.22, 0.18)
    return jnp.clip(result, -most, most).astype(dtype)


def setup_inputs(seed: int = 0) -> dict:
    keys = jax.random.split(jax.random.key(seed), 12)
    leaf_out = scatter_about(keys[0], (2, LEAVES, K0), 1.0, 6.0, ((1, 32),))
    interp_mid = scatter_about(keys[1], (K0, K1), K0 ** -0.5, 0.1875)
    shift_mid = jnp.clip(jax.random.uniform(keys[2], (8, K1), jnp.float32, -3.140625, 3.140625), -3.140625, 3.140625)
    trans_mid = scatter_about(keys[3], (2, NOFF, K1), (2 * NLIST) ** -0.5, 0.5, ((2, 8),), jnp.float32)
    list_mid = with_ends(jax.random.randint(keys[4], (MID_BOXES, NLIST), 0, MID_BOXES), jax.random.fold_in(keys[4], 1), 0, MID_BOXES - 1).astype(jnp.int32)
    offset_mid = with_ends(jax.random.randint(keys[5], (MID_BOXES, NLIST), 0, NOFF), jax.random.fold_in(keys[5], 1), 0, NOFF - 1).astype(jnp.int32)
    interp_top = scatter_about(keys[6], (SECT, K1_SECT, K2_SECT), K1_SECT ** -0.5, 0.25, ((0, 8),))
    shift_top = jnp.clip(jax.random.uniform(keys[7], (8, SECT, K2_SECT), jnp.float32, -3.140625, 3.140625), -3.140625, 3.140625)
    trans_top = scatter_about(keys[8], (2, NOFF, SECT, K2_SECT), (2 * NLIST) ** -0.5, 0.5, ((2, 8), (3, 4)), jnp.float32)
    list_top = with_ends(jax.random.randint(keys[9], (TOP_BOXES, NLIST), 0, TOP_BOXES), jax.random.fold_in(keys[9], 1), 0, TOP_BOXES - 1).astype(jnp.int32)
    offset_top = with_ends(jax.random.randint(keys[10], (TOP_BOXES, NLIST), 0, NOFF), jax.random.fold_in(keys[10], 1), 0, NOFF - 1).astype(jnp.int32)
    return {"leaf_out": leaf_out, "interp_mid": interp_mid, "shift_mid": shift_mid, "trans_mid": trans_mid, "list_mid": list_mid, "offset_mid": offset_mid, "interp_top": interp_top, "shift_top": shift_top, "trans_top": trans_top, "list_top": list_top, "offset_top": offset_top}


def complex_translate(patterns, sources, offsets, operators, block_rows):
    row_count = sources.shape[0]
    source_blocks = sources.reshape(row_count // block_rows, block_rows, sources.shape[1])
    offset_blocks = offsets.reshape(row_count // block_rows, block_rows, offsets.shape[1])

    def one_block(indices):
        picked = jnp.take(patterns, indices[0], axis=1).astype(jnp.float32)
        factors = jnp.take(operators, indices[1], axis=1).astype(jnp.float32)
        real_part = jnp.sum(picked[0] * factors[0] - picked[1] * factors[1], axis=1)
        imag_part = jnp.sum(picked[0] * factors[1] + picked[1] * factors[0], axis=1)
        return jnp.stack([real_part, imag_part])

    blocks = lax.map(one_block, (source_blocks, offset_blocks))
    return jnp.transpose(blocks, (1, 0, 2, 3)).reshape(2, row_count, patterns.shape[2])


def aggregate(patterns, matrix, cos_table, sin_table):
    real_part = jnp.dot(patterns[0], matrix, preferred_element_type=jnp.float32)
    imag_part = jnp.dot(patterns[1], matrix, preferred_element_type=jnp.float32)
    parent_count = patterns.shape[1] // 8
    real_part = real_part.reshape(parent_count, 8, matrix.shape[1])
    imag_part = imag_part.reshape(parent_count, 8, matrix.shape[1])
    summed_real = jnp.sum(real_part * cos_table[None] - imag_part * sin_table[None], axis=1)
    summed_imag = jnp.sum(real_part * sin_table[None] + imag_part * cos_table[None], axis=1)
    return jnp.stack([summed_real, summed_imag]).astype(jnp.bfloat16)


def child_shift(parents, cos_table, sin_table):
    real_part = parents[0].astype(jnp.float32)[:, None, :]
    imag_part = parents[1].astype(jnp.float32)[:, None, :]
    new_real = real_part * cos_table[None] + imag_part * sin_table[None]
    new_imag = imag_part * cos_table[None] - real_part * sin_table[None]
    return jnp.stack([new_real, new_imag]).reshape(2, -1, cos_table.shape[1]).astype(jnp.bfloat16)


def adjoint_apply(children, matrix):
    dims = (((1,), (1,)), ((), ()))
    real_part = lax.dot_general(children[0], matrix, dims, preferred_element_type=jnp.float32)
    imag_part = lax.dot_general(children[1], matrix, dims, preferred_element_type=jnp.float32)
    return jnp.stack([real_part, imag_part])


def reference(leaf_out, interp_mid, shift_mid, trans_mid, list_mid, offset_mid, interp_top, shift_top, trans_top, list_top, offset_top):
    cos_mid = jnp.cos(shift_mid)
    sin_mid = jnp.sin(shift_mid)
    leaf_blocks = jnp.transpose(leaf_out.reshape(2, LEAVES // LEAF_DEV, LEAF_DEV, K0), (1, 0, 2, 3))
    mid_blocks = lax.map(lambda part: aggregate(part, interp_mid, cos_mid, sin_mid), leaf_blocks)
    mid_pattern = jnp.transpose(mid_blocks, (1, 0, 2, 3)).reshape(2, MID_BOXES, K1)
    mid_far = complex_translate(mid_pattern, list_mid, offset_mid, trans_mid, math.gcd(MID_BOXES, 16))
    sector_in = jnp.transpose(mid_pattern.reshape(2, MID_BOXES, SECT, K1_SECT), (2, 0, 1, 3))
    cos_top = jnp.transpose(jnp.cos(shift_top), (1, 0, 2))
    sin_top = jnp.transpose(jnp.sin(shift_top), (1, 0, 2))
    top_blocks = lax.map(lambda item: aggregate(item[0], item[1], item[2], item[3]), (sector_in, interp_top, cos_top, sin_top))
    top_pattern = jnp.transpose(top_blocks, (1, 2, 0, 3)).reshape(2, TOP_BOXES, K2)
    top_in = complex_translate(top_pattern, list_top, offset_top, trans_top.reshape(2, NOFF, K2), math.gcd(TOP_BOXES, 4)).astype(jnp.bfloat16)
    top_sectors = jnp.transpose(top_in.reshape(2, TOP_BOXES, SECT, K2_SECT), (2, 0, 1, 3))

    def descend(item):
        children = child_shift(item[0], item[2], item[3])
        return adjoint_apply(children, item[1]) * (K1_SECT / K2_SECT)

    down_blocks = lax.map(descend, (top_sectors, interp_top, cos_top, sin_top))
    down_top = jnp.transpose(down_blocks, (1, 2, 0, 3)).reshape(2, MID_BOXES, K1)
    mid_in = (mid_far + down_top).astype(jnp.bfloat16)
    parent_blocks = jnp.transpose(mid_in.reshape(2, LEAVES // LEAF_DEV, LEAF_DEV // 8, K1), (1, 0, 2, 3))
    leaf_blocks_in = lax.map(lambda part: adjoint_apply(child_shift(part, cos_mid, sin_mid), interp_mid), parent_blocks)
    leaf_in = jnp.transpose(leaf_blocks_in, (1, 0, 2, 3)).reshape(2, LEAVES, K0)
    return leaf_in * (K0 / K1)
```

```python
import functools

import jax
import jax.numpy as jnp
from jax import lax
from jax.experimental import pallas as pl
from jax.experimental.pallas import tpu as pltpu
from jax.sharding import PartitionSpec as P

SINE = (1.0, -0.16666647791862488, 0.00833289884030819, -0.0001980085507966578, 2.5904087124217767e-06)
COSINE = (1.0, -0.5, 0.04166663438081741, -0.0013888360699638724, 2.476012559782248e-05, -2.6050881274386484e-07)
LANES = 128
ROWS = 8
VMEM_BYTES = 48 * 1024 * 1024


def powers(square, factors):
    total = jnp.full_like(square, factors[-1])
    for factor in factors[-2::-1]:
        total = total * square + factor
    return total


def phase(angle):
    half = angle * 0.5
    square = half * half
    sine = half * powers(square, SINE)
    cosine = powers(square, COSINE)
    return 1.0 - 2.0 * sine * sine, 2.0 * sine * cosine


def leaf_up(leaf_ref, table_ref, shift_ref, out_ref):
    octants, width = shift_ref.shape
    values = jnp.dot(leaf_ref[...], table_ref[...], preferred_element_type=jnp.float32)
    leaves = values.shape[0] // 2
    real = values[:leaves].reshape(leaves // octants, octants, width)
    imag = values[leaves:].reshape(leaves // octants, octants, width)
    cos, sin = phase(shift_ref[...])
    new_real = jnp.sum(real * cos[None] - imag * sin[None], axis=1)
    new_imag = jnp.sum(real * sin[None] + imag * cos[None], axis=1)
    block = jnp.concatenate([new_real, new_imag], axis=0).astype(out_ref.dtype)
    for copy in range(out_ref.shape[0]):
        out_ref[copy, 0] = block


def spread_rows(block, plain_ref, swapped_ref, first, part):
    pieces = block.shape[1] // LANES
    height = 2 * pieces
    for piece in range(pieces):
        lanes = block[:, piece * LANES : (piece + 1) * LANES]
        plain_ref[pl.ds(first * height + 2 * piece + part, ROWS, stride=height), :] = lanes
        swapped_ref[pl.ds(first * height + 2 * piece + 1 - part, ROWS, stride=height), :] = lanes


def translate(source_ref, offset_ref, trans_ref, plain_ref, swapped_ref, same_ref, cross_ref, row_count, height):
    list_width = source_ref.shape[0] // row_count

    def one_row(row, carry):
        same = [jnp.zeros((height, LANES), jnp.float32) for _ in range(2)]
        cross = [jnp.zeros((height, LANES), jnp.float32) for _ in range(2)]
        for entry in range(list_width):
            at = row * list_width + entry
            offset = pl.ds(pl.multiple_of(offset_ref[at], height), height)
            source = pl.ds(pl.multiple_of(source_ref[at], height), height)
            factor = trans_ref[offset, :]
            same[entry % 2] += factor * plain_ref[source, :]
            cross[entry % 2] += factor * swapped_ref[source, :]
        place = pl.ds(pl.multiple_of(row * height, height), height)
        same_ref[place, :] = same[0] + same[1]
        cross_ref[place, :] = cross[0] + cross[1]
        return carry

    lax.fori_loop(0, row_count, one_row, 0)


def gather_rows(same_ref, cross_ref, first, height):
    real, imag = [], []
    for piece in range(height // 2):
        even = pl.ds(first * height + 2 * piece, ROWS, stride=height)
        odd = pl.ds(first * height + 2 * piece + 1, ROWS, stride=height)
        real.append(same_ref[even, :] - same_ref[odd, :])
        imag.append(cross_ref[even, :] + cross_ref[odd, :])
    return jnp.concatenate(real, axis=1), jnp.concatenate(imag, axis=1)


def mid_translate(source_ref, offset_ref, mid_ref, trans_ref, out_ref, plain_ref, swapped_ref, same_ref, cross_ref):
    blocks, _, width = mid_ref.shape
    height = 2 * width // LANES
    for block in range(blocks):
        rows = mid_ref[block].astype(jnp.float32)
        spread_rows(rows[:ROWS], plain_ref, swapped_ref, block * ROWS, 0)
        spread_rows(rows[ROWS:], plain_ref, swapped_ref, block * ROWS, 1)
    row_count = out_ref.shape[1]
    translate(source_ref, offset_ref, trans_ref, plain_ref, swapped_ref, same_ref, cross_ref, row_count, height)
    for first in range(0, row_count, ROWS):
        real, imag = gather_rows(same_ref, cross_ref, first, height)
        out_ref[0, first : first + ROWS] = real
        out_ref[1, first : first + ROWS] = imag


def top_level(box_ref, source_ref, offset_ref, mid_ref, table_ref, shift_ref, trans_ref, out_ref, plain_ref, swapped_ref, same_ref, cross_ref):
    blocks, double, _ = mid_ref.shape
    octants, width = shift_ref.shape
    height = 2 * width // LANES
    cos, sin = phase(shift_ref[...])
    for first in range(0, blocks, ROWS):
        group = mid_ref[first : first + ROWS].reshape(ROWS * double, mid_ref.shape[2])
        values = jnp.dot(group, table_ref[0], preferred_element_type=jnp.float32)
        values = values.reshape(ROWS, double, width)
        real, imag = values[:, :octants], values[:, octants:]
        new_real = jnp.sum(real * cos[None] - imag * sin[None], axis=1)
        new_imag = jnp.sum(real * sin[None] + imag * cos[None], axis=1)
        new_real = new_real.astype(jnp.bfloat16).astype(jnp.float32)
        new_imag = new_imag.astype(jnp.bfloat16).astype(jnp.float32)
        spread_rows(new_real, plain_ref, swapped_ref, first, 0)
        spread_rows(new_imag, plain_ref, swapped_ref, first, 1)
    translate(source_ref, offset_ref, trans_ref, plain_ref, swapped_ref, same_ref, cross_ref, blocks, height)
    groups, own, _ = out_ref.shape
    own = own // 2
    for group in range(groups):
        real, imag = [], []
        for first in range(0, own, ROWS):
            new_real, new_imag = gather_rows(same_ref, cross_ref, group * own + first, height)
            real.append(new_real)
            imag.append(new_imag)
        out_ref[group] = jnp.concatenate(real + imag, axis=0).astype(out_ref.dtype)


def children_of(parents, cos, sin):
    half = parents.shape[0] // 2
    octants, width = cos.shape
    parents = parents.astype(jnp.float32)
    real, imag = parents[:half, None, :], parents[half:, None, :]
    new_real = (real * cos[None] + imag * sin[None]).reshape(half * octants, width)
    new_imag = (imag * cos[None] - real * sin[None]).reshape(half * octants, width)
    return jnp.concatenate([new_real, new_imag], axis=0).astype(jnp.bfloat16)


ADJOINT = (((1,), (1,)), ((), ()))


def top_down(scale, top_ref, table_ref, shift_ref, far_ref, out_ref):
    slices, double, width = top_ref.shape
    total = None
    for part in range(slices):
        columns = slice(part * width, (part + 1) * width)
        cos, sin = phase(shift_ref[:, columns])
        children = children_of(top_ref[part], cos, sin)
        term = lax.dot_general(children, table_ref[0, :, columns], ADJOINT, preferred_element_type=jnp.float32)
        total = term if total is None else total + term
    half = total.shape[0] // 2
    real = far_ref[0] + scale * total[:half]
    imag = far_ref[1] + scale * total[half:]
    owners, rows, _ = out_ref.shape
    rows = rows // 2
    for owner in range(owners):
        place = slice(owner * rows, (owner + 1) * rows)
        out_ref[owner] = jnp.concatenate([real[place], imag[place]], axis=0).astype(out_ref.dtype)


def leaf_down(scale, mid_ref, table_ref, shift_ref, out_ref):
    step = pl.program_id(0)
    cos, sin = phase(shift_ref[...])
    children = children_of(mid_ref[0], cos, sin)
    term = lax.dot_general(children, table_ref[...], ADJOINT, preferred_element_type=jnp.float32) * scale

    @pl.when(step == 0)
    def _():
        out_ref[...] = term

    @pl.when(step > 0)
    def _():
        out_ref[...] += term


def params():
    return pltpu.CompilerParams(vmem_limit_bytes=VMEM_BYTES)


def rows_of(trans):
    _, offsets, width = trans.shape
    pieces = width // LANES
    rows = jnp.transpose(trans.reshape(2, offsets, pieces, LANES), (1, 2, 0, 3))
    return rows.reshape(offsets * pieces * 2, LANES)


def on_device(
    leaf_out,
    interp_mid,
    shift_mid,
    trans_mid,
    list_mid,
    offset_mid,
    interp_top,
    shift_top,
    trans_top,
    list_top,
    offset_top,
):
    boxes = lax.axis_size("box")
    dirs = lax.axis_size("dir")
    box_index = lax.axis_index("box")
    octants = shift_mid.shape[0]
    leaves = leaf_out.shape[1]
    leaf_width, mid_width = interp_mid.shape
    own_mids = leaves // octants
    sector = trans_mid.shape[2]
    top_sector = interp_top.shape[2]
    top_width = trans_top.shape[3]
    devices = boxes * dirs
    mids = list_mid.shape[0]
    group_mids = mids // boxes
    tops = list_top.shape[0]
    group_tops = tops // boxes
    vmem = pl.BlockSpec(memory_space=pltpu.VMEM)
    smem = pl.BlockSpec(memory_space=pltpu.SMEM)

    outgoing = pl.pallas_call(
        leaf_up,
        grid=(dirs,),
        in_specs=[
            pl.BlockSpec((2 * leaves, leaf_width), lambda s: (0, 0)),
            pl.BlockSpec((leaf_width, sector), lambda s: (0, s)),
            pl.BlockSpec((octants, sector), lambda s: (0, s)),
        ],
        out_specs=pl.BlockSpec((boxes, 1, 2 * own_mids, sector), lambda s: (0, s, 0, 0)),
        out_shape=jax.ShapeDtypeStruct((boxes, dirs, 2 * own_mids, sector), jnp.bfloat16),
        compiler_params=params(),
        name="leaf_up",
    )(leaf_out.reshape(2 * leaves, leaf_width), interp_mid, shift_mid)
    outgoing = outgoing.reshape(devices, 2 * own_mids, sector)
    mid_all = lax.all_to_all(outgoing, ("box", "dir"), split_axis=0, concat_axis=0, tiled=True)

    top_height = 2 * top_width // LANES
    box_scalar = box_index.astype(jnp.int32).reshape(1)
    top_in = pl.pallas_call(
        top_level,
        grid_spec=pltpu.PrefetchScalarGridSpec(
            num_scalar_prefetch=3,
            grid=(1,),
            in_specs=[
                pl.BlockSpec(mid_all.shape, lambda i, box, *_: (0, 0, 0)),
                pl.BlockSpec((1, sector, top_width), lambda i, box, *_: (0, 0, box[0])),
                pl.BlockSpec((octants, top_width), lambda i, box, *_: (0, box[0])),
                pl.BlockSpec((trans_top.shape[1] * top_height, LANES), lambda i, box, *_: (0, 0)),
            ],
            out_specs=pl.BlockSpec((boxes, 2 * group_tops, top_width), lambda i, box, *_: (0, 0, 0)),
            scratch_shapes=[pltpu.VMEM((tops * top_height, LANES), jnp.float32)] * 4,
        ),
        out_shape=jax.ShapeDtypeStruct((boxes, 2 * group_tops, top_width), jnp.bfloat16),
        compiler_params=params(),
        name="top_level",
    )(
        box_scalar,
        (list_top * top_height).reshape(-1),
        (offset_top * top_height).reshape(-1),
        mid_all,
        interp_top,
        shift_top.reshape(octants, top_sector),
        rows_of(trans_top.reshape(2, -1, top_width)),
    )
    top_back = lax.all_to_all(top_in, "box", split_axis=0, concat_axis=0, tiled=True)

    mid_height = 2 * sector // LANES
    own_list = lax.dynamic_slice_in_dim(list_mid, box_index * group_mids, group_mids, 0)
    own_offsets = lax.dynamic_slice_in_dim(offset_mid, box_index * group_mids, group_mids, 0)
    mid_far = pl.pallas_call(
        mid_translate,
        in_specs=[smem, smem, vmem, vmem],
        out_specs=vmem,
        out_shape=jax.ShapeDtypeStruct((2, group_mids, sector), jnp.float32),
        scratch_shapes=[pltpu.VMEM((mids * mid_height, LANES), jnp.float32)] * 2
        + [pltpu.VMEM((group_mids * mid_height, LANES), jnp.float32)] * 2,
        compiler_params=params(),
        name="mid_translate",
    )(
        (own_list * mid_height).reshape(-1),
        (own_offsets * mid_height).reshape(-1),
        mid_all,
        rows_of(trans_mid),
    )

    incoming = pl.pallas_call(
        functools.partial(top_down, sector / top_sector),
        in_specs=[vmem] * 4,
        out_specs=vmem,
        out_shape=jax.ShapeDtypeStruct((dirs, 2 * own_mids, sector), jnp.bfloat16),
        compiler_params=params(),
        name="top_down",
    )(top_back, interp_top, shift_top.reshape(octants, top_sector), mid_far)
    mid_back = lax.all_to_all(incoming, "dir", split_axis=0, concat_axis=0, tiled=True)

    leaf_in = pl.pallas_call(
        functools.partial(leaf_down, leaf_width / mid_width),
        grid=(dirs,),
        in_specs=[
            pl.BlockSpec((1, 2 * own_mids, sector), lambda s: (s, 0, 0)),
            pl.BlockSpec((leaf_width, sector), lambda s: (0, s)),
            pl.BlockSpec((octants, sector), lambda s: (0, s)),
        ],
        out_specs=pl.BlockSpec((2 * leaves, leaf_width), lambda s: (0, 0)),
        out_shape=jax.ShapeDtypeStruct((2 * leaves, leaf_width), jnp.float32),
        compiler_params=params(),
        name="leaf_down",
    )(mid_back, interp_mid, shift_mid)
    return leaf_in.reshape(2, leaves, leaf_width)


def solution(mesh):
    return jax.shard_map(
        on_device,
        mesh=mesh,
        in_specs=(
            P(None, ("box", "dir"), None),
            P(),
            P(),
            P(None, None, "dir"),
            P(),
            P(),
            P("dir", None, None),
            P(None, "dir", None),
            P(None, None, "dir", "box"),
            P(),
            P(),
        ),
        out_specs=P(None, ("box", "dir"), None),
        check_vma=False,
    )
```

```python
import functools
import math

import jax
import jax.numpy as jnp
from jax import lax
from jax.experimental import pallas as pl
from jax.experimental.pallas import tpu as pltpu
from jax.sharding import PartitionSpec as P

SINE = (1.0, -0.16666647791862488, 0.00833289884030819, -0.0001980085507966578, 2.5904087124217767e-06)
COSINE = (1.0, -0.5, 0.04166663438081741, -0.0013888360699638724, 2.476012559782248e-05, -2.6050881274386484e-07)
LANES = 128
ROWS = 8
AHEAD = 2
CHUNK_SECTORS = 2


def powers(square, factors):
    total = jnp.full_like(square, factors[-1])
    for factor in factors[-2::-1]:
        total = total * square + factor
    return total


def phase(angle):
    half = angle * 0.5
    square = half * half
    sine = half * powers(square, SINE)
    cosine = powers(square, COSINE)
    return 1.0 - 2.0 * sine * sine, 2.0 * sine * cosine


def leaf_up(leaf_hbm, table_hbm, shift_hbm, out_ref, leaf_ref, shift_ref, table_ref, small_sems, table_sems):
    chunks, _, width = table_ref.shape
    octants = shift_ref.shape[0]
    copies, _, rows, sector = out_ref.shape
    leaf_copy = pltpu.make_async_copy(leaf_hbm, leaf_ref, small_sems.at[0])
    shift_copy = pltpu.make_async_copy(shift_hbm, shift_ref, small_sems.at[1])

    def table_copy(chunk):
        source = table_hbm.at[:, pl.ds(chunk * width, width)]
        return pltpu.make_async_copy(source, table_ref.at[chunk], table_sems.at[chunk])

    leaf_copy.start()
    table_copy(0).start()
    shift_copy.start()
    for chunk in range(1, min(AHEAD, chunks)):
        table_copy(chunk).start()
    leaf_copy.wait()
    shift_copy.wait()
    leaves = leaf_ref.shape[0] // 2
    for chunk in range(chunks):
        table_copy(chunk).wait()
        if chunk + AHEAD < chunks:
            table_copy(chunk + AHEAD).start()
        values = jnp.dot(leaf_ref[...], table_ref[chunk], preferred_element_type=jnp.float32)
        real = values[:leaves].reshape(leaves // octants, octants, width)
        imag = values[leaves:].reshape(leaves // octants, octants, width)
        cos, sin = phase(shift_ref[:, chunk * width : (chunk + 1) * width])
        new_real = jnp.sum(real * cos[None] - imag * sin[None], axis=1)
        new_imag = jnp.sum(real * sin[None] + imag * cos[None], axis=1)
        block = jnp.concatenate([new_real, new_imag], axis=0).astype(out_ref.dtype)
        for part in range(width // sector):
            for copy in range(copies):
                out_ref[copy, chunk * (width // sector) + part] = block[:, part * sector : (part + 1) * sector]


def spread_rows(block, pattern_ref, first, part):
    pieces = block.shape[1] // LANES
    height = 2 * pieces
    for piece in range(pieces):
        lanes = block[:, piece * LANES : (piece + 1) * LANES]
        start = 2 * first * height + 2 * piece
        pattern_ref[pl.ds(start + part, ROWS, stride=2 * height), :] = lanes
        pattern_ref[pl.ds(start + height + 1 - part, ROWS, stride=2 * height), :] = lanes


def translate(source_ref, offset_ref, trans_ref, pattern_ref, same_ref, cross_ref, row_count, height):
    list_width = source_ref.shape[0] // row_count

    def one_row(row, carry):
        same = [jnp.zeros((height, LANES), jnp.float32) for _ in range(2)]
        cross = [jnp.zeros((height, LANES), jnp.float32) for _ in range(2)]
        for entry in range(list_width):
            at = row * list_width + entry
            offset = pl.multiple_of(offset_ref[at], height)
            source = pl.multiple_of(source_ref[at], height)
            factor = trans_ref[pl.ds(offset, height), :]
            same[entry % 2] += factor * pattern_ref[pl.ds(source, height), :]
            cross[entry % 2] += factor * pattern_ref[pl.ds(source + height, height), :]
        place = pl.ds(pl.multiple_of(row * height, height), height)
        same_ref[place, :] = same[0] + same[1]
        cross_ref[place, :] = cross[0] + cross[1]
        return carry

    lax.fori_loop(0, row_count, one_row, 0)


def gather_rows(same_ref, cross_ref, first, height):
    real, imag = [], []
    for piece in range(height // 2):
        even = pl.ds(first * height + 2 * piece, ROWS, stride=height)
        odd = pl.ds(first * height + 2 * piece + 1, ROWS, stride=height)
        real.append(same_ref[even, :] - same_ref[odd, :])
        imag.append(cross_ref[even, :] + cross_ref[odd, :])
    return jnp.concatenate(real, axis=1), jnp.concatenate(imag, axis=1)


def mid_translate(source_ref, offset_ref, mid_ref, trans_ref, out_ref, pattern_ref, same_ref, cross_ref):
    blocks, _, width = mid_ref.shape
    height = 2 * width // LANES
    for block in range(blocks):
        rows = mid_ref[block].astype(jnp.float32)
        spread_rows(rows[:ROWS], pattern_ref, block * ROWS, 0)
        spread_rows(rows[ROWS:], pattern_ref, block * ROWS, 1)
    row_count = out_ref.shape[1]
    translate(source_ref, offset_ref, trans_ref, pattern_ref, same_ref, cross_ref, row_count, height)
    for first in range(0, row_count, ROWS):
        real, imag = gather_rows(same_ref, cross_ref, first, height)
        out_ref[0, first : first + ROWS] = real
        out_ref[1, first : first + ROWS] = imag


def top_level(box_ref, source_ref, offset_ref, mid_ref, table_ref, shift_ref, trans_ref, out_ref, pattern_ref, same_ref, cross_ref):
    blocks, double, _ = mid_ref.shape
    octants = shift_ref.shape[0]
    width = out_ref.shape[2]
    height = 2 * width // LANES
    columns = pl.ds(pl.multiple_of(box_ref[0] * width, width), width)
    cos, sin = phase(shift_ref[:, columns])
    for first in range(0, blocks, ROWS):
        group = mid_ref[first : first + ROWS].reshape(ROWS * double, mid_ref.shape[2])
        values = jnp.dot(group, table_ref[0, :, columns], preferred_element_type=jnp.float32)
        values = values.reshape(ROWS, double, width)
        real, imag = values[:, :octants], values[:, octants:]
        new_real = jnp.sum(real * cos[None] - imag * sin[None], axis=1)
        new_imag = jnp.sum(real * sin[None] + imag * cos[None], axis=1)
        new_real = new_real.astype(jnp.bfloat16).astype(jnp.float32)
        new_imag = new_imag.astype(jnp.bfloat16).astype(jnp.float32)
        spread_rows(new_real, pattern_ref, first, 0)
        spread_rows(new_imag, pattern_ref, first, 1)
    translate(source_ref, offset_ref, trans_ref, pattern_ref, same_ref, cross_ref, blocks, height)
    groups, own, _ = out_ref.shape
    own = own // 2
    for group in range(groups):
        real, imag = [], []
        for first in range(0, own, ROWS):
            new_real, new_imag = gather_rows(same_ref, cross_ref, group * own + first, height)
            real.append(new_real)
            imag.append(new_imag)
        out_ref[group] = jnp.concatenate(real + imag, axis=0).astype(out_ref.dtype)


def children_of(parents, cos, sin):
    half = parents.shape[0] // 2
    octants, width = cos.shape
    parents = parents.astype(jnp.float32)
    real, imag = parents[:half, None, :], parents[half:, None, :]
    new_real = (real * cos[None] + imag * sin[None]).reshape(half * octants, width)
    new_imag = (imag * cos[None] - real * sin[None]).reshape(half * octants, width)
    return jnp.concatenate([new_real, new_imag], axis=0).astype(jnp.bfloat16)


ADJOINT = (((1,), (1,)), ((), ()))


def top_down(scale, top_ref, table_ref, shift_ref, far_ref, out_ref):
    slices, double, width = top_ref.shape
    total = None
    for part in range(slices):
        columns = slice(part * width, (part + 1) * width)
        cos, sin = phase(shift_ref[:, columns])
        children = children_of(top_ref[part], cos, sin)
        term = lax.dot_general(children, table_ref[0, :, columns], ADJOINT, preferred_element_type=jnp.float32)
        total = term if total is None else total + term
    half = total.shape[0] // 2
    real = far_ref[0] + scale * total[:half]
    imag = far_ref[1] + scale * total[half:]
    owners, rows, _ = out_ref.shape
    rows = rows // 2
    for owner in range(owners):
        place = slice(owner * rows, (owner + 1) * rows)
        out_ref[owner] = jnp.concatenate([real[place], imag[place]], axis=0).astype(out_ref.dtype)


def leaf_down(scale, mid_ref, table_ref, shift_ref, out_ref, total_ref):
    sectors, _, width = mid_ref.shape
    for part in range(sectors):
        columns = slice(part * width, (part + 1) * width)
        cos, sin = phase(shift_ref[:, columns])
        children = children_of(mid_ref[part], cos, sin)
        term = lax.dot_general(table_ref[:, columns], children, ADJOINT, preferred_element_type=jnp.float32)
        if part == 0:
            total_ref[...] = term
        else:
            total_ref[...] += term
    out_ref[...] = total_ref[...].T * scale


def params(mebibytes):
    return pltpu.CompilerParams(vmem_limit_bytes=mebibytes * 1024 * 1024)


def rows_of(trans):
    _, offsets, width = trans.shape
    pieces = width // LANES
    rows = jnp.transpose(trans.reshape(2, offsets, pieces, LANES), (1, 2, 0, 3))
    return rows.reshape(offsets * pieces * 2, LANES)


def on_device(
    leaf_out,
    interp_mid,
    shift_mid,
    trans_mid,
    list_mid,
    offset_mid,
    interp_top,
    shift_top,
    trans_top,
    list_top,
    offset_top,
):
    boxes = lax.axis_size("box")
    dirs = lax.axis_size("dir")
    box_index = lax.axis_index("box")
    octants = shift_mid.shape[0]
    leaves = leaf_out.shape[1]
    leaf_width, mid_width = interp_mid.shape
    own_mids = leaves // octants
    sector = trans_mid.shape[2]
    top_sector = interp_top.shape[2]
    top_width = trans_top.shape[3]
    devices = boxes * dirs
    mids = list_mid.shape[0]
    group_mids = mids // boxes
    tops = list_top.shape[0]
    group_tops = tops // boxes
    vmem = pl.BlockSpec(memory_space=pltpu.VMEM)
    smem = pl.BlockSpec(memory_space=pltpu.SMEM)
    hbm = pl.BlockSpec(memory_space=pl.ANY)
    top_height = 2 * top_width // LANES
    mid_height = 2 * sector // LANES

    chunk = sector * math.gcd(dirs, CHUNK_SECTORS)
    chunks = mid_width // chunk
    outgoing = pl.pallas_call(
        leaf_up,
        in_specs=[hbm, hbm, hbm],
        out_specs=vmem,
        out_shape=jax.ShapeDtypeStruct((boxes, dirs, 2 * own_mids, sector), jnp.bfloat16),
        scratch_shapes=[
            pltpu.VMEM((2 * leaves, leaf_width), jnp.bfloat16),
            pltpu.VMEM((octants, mid_width), jnp.float32),
            pltpu.VMEM((chunks, leaf_width, chunk), jnp.bfloat16),
            pltpu.SemaphoreType.DMA((2,)),
            pltpu.SemaphoreType.DMA((chunks,)),
        ],
        compiler_params=params(60),
        name="leaf_up",
    )(leaf_out.reshape(2 * leaves, leaf_width), interp_mid, shift_mid)
    outgoing = outgoing.reshape(devices, 2 * own_mids, sector)
    mid_all = lax.all_to_all(outgoing, ("box", "dir"), split_axis=0, concat_axis=0, tiled=True)

    box_scalar = box_index.astype(jnp.int32).reshape(1)
    top_list = (list_top * (2 * top_height)).reshape(-1)
    top_offsets = (offset_top * top_height).reshape(-1)
    own_list = lax.dynamic_slice_in_dim(list_mid, box_index * group_mids, group_mids, 0)
    own_offsets = lax.dynamic_slice_in_dim(offset_mid, box_index * group_mids, group_mids, 0)
    own_list = (own_list * (2 * mid_height)).reshape(-1)
    own_offsets = (own_offsets * mid_height).reshape(-1)
    rows_top = rows_of(trans_top.reshape(2, -1, top_width))
    rows_mid = rows_of(trans_mid)
    angles_top = shift_top.reshape(octants, top_sector)
    ready = (mid_all, top_list, top_offsets, own_list, own_offsets, rows_top, rows_mid, angles_top)
    mid_all, top_list, top_offsets, own_list, own_offsets, rows_top, rows_mid, angles_top = lax.optimization_barrier(ready)

    top_in = pl.pallas_call(
        top_level,
        in_specs=[smem, smem, smem, vmem, vmem, vmem, vmem],
        out_specs=vmem,
        out_shape=jax.ShapeDtypeStruct((boxes, 2 * group_tops, top_width), jnp.bfloat16),
        scratch_shapes=[
            pltpu.VMEM((2 * tops * top_height, LANES), jnp.float32),
            pltpu.VMEM((tops * top_height, LANES), jnp.float32),
            pltpu.VMEM((tops * top_height, LANES), jnp.float32),
        ],
        compiler_params=params(16),
        name="top_level",
    )(box_scalar, top_list, top_offsets, mid_all, interp_top, angles_top, rows_top)
    top_back = lax.all_to_all(top_in, "box", split_axis=0, concat_axis=0, tiled=True)

    mid_far = pl.pallas_call(
        mid_translate,
        in_specs=[smem, smem, vmem, vmem],
        out_specs=vmem,
        out_shape=jax.ShapeDtypeStruct((2, group_mids, sector), jnp.float32),
        scratch_shapes=[
            pltpu.VMEM((2 * mids * mid_height, LANES), jnp.float32),
            pltpu.VMEM((group_mids * mid_height, LANES), jnp.float32),
            pltpu.VMEM((group_mids * mid_height, LANES), jnp.float32),
        ],
        compiler_params=params(16),
        name="mid_translate",
    )(own_list, own_offsets, mid_all, rows_mid)

    incoming = pl.pallas_call(
        functools.partial(top_down, sector / top_sector),
        in_specs=[vmem] * 4,
        out_specs=vmem,
        out_shape=jax.ShapeDtypeStruct((dirs, 2 * own_mids, sector), jnp.bfloat16),
        compiler_params=params(16),
        name="top_down",
    )(top_back, interp_top, angles_top, mid_far)
    mid_back = lax.all_to_all(incoming, "dir", split_axis=0, concat_axis=0, tiled=True)

    leaf_in = pl.pallas_call(
        functools.partial(leaf_down, leaf_width / mid_width),
        in_specs=[vmem] * 3,
        out_specs=vmem,
        out_shape=jax.ShapeDtypeStruct((2 * leaves, leaf_width), jnp.float32),
        scratch_shapes=[pltpu.VMEM((leaf_width, 2 * leaves), jnp.float32)],
        compiler_params=params(20),
        name="leaf_down",
    )(mid_back, interp_mid, shift_mid)
    return leaf_in.reshape(2, leaves, leaf_width)


def solution(mesh):
    return jax.shard_map(
        on_device,
        mesh=mesh,
        in_specs=(
            P(None, ("box", "dir"), None),
            P(),
            P(),
            P(None, None, "dir"),
            P(),
            P(),
            P("dir", None, None),
            P(None, "dir", None),
            P(None, None, "dir", "box"),
            P(),
            P(),
        ),
        out_specs=P(None, ("box", "dir"), None),
        check_vma=False,
    )
```

```python
import functools
import math

import jax
import jax.numpy as jnp
from jax import lax
from jax.experimental import pallas as pl
from jax.experimental.pallas import tpu as pltpu
from jax.sharding import PartitionSpec as P

SINE = (1.0, -0.16666647791862488, 0.00833289884030819, -0.0001980085507966578, 2.5904087124217767e-06)
COSINE = (1.0, -0.5, 0.04166663438081741, -0.0013888360699638724, 2.476012559782248e-05, -2.6050881274386484e-07)
HEAD_ROWS = 4
LANES = 128
ROWS = 8
AHEAD = 2
CHUNK_SECTORS = 2


def powers(square, factors):
    total = jnp.full_like(square, factors[-1])
    for factor in factors[-2::-1]:
        total = total * square + factor
    return total


def phase(angle):
    half = angle * 0.5
    square = half * half
    sine = half * powers(square, SINE)
    cosine = powers(square, COSINE)
    return 1.0 - 2.0 * sine * sine, 2.0 * sine * cosine


def leaf_up(leaf_hbm, table_hbm, shift_hbm, out_ref, leaf_ref, shift_ref, table_ref, small_sems, table_sems):
    chunks, _, width = table_ref.shape
    octants = shift_ref.shape[0]
    sector = out_ref.shape[2]
    leaf_copy = pltpu.make_async_copy(leaf_hbm, leaf_ref, small_sems.at[0])
    shift_copy = pltpu.make_async_copy(shift_hbm, shift_ref, small_sems.at[1])

    def table_copy(chunk):
        source = table_hbm.at[:, pl.ds(chunk * width, width)]
        return pltpu.make_async_copy(source, table_ref.at[chunk], table_sems.at[chunk])

    leaf_copy.start()
    table_copy(0).start()
    shift_copy.start()
    for chunk in range(1, min(AHEAD, chunks)):
        table_copy(chunk).start()
    leaf_copy.wait()
    shift_copy.wait()
    leaves = leaf_ref.shape[0] // 2
    for chunk in range(chunks):
        table_copy(chunk).wait()
        if chunk + AHEAD < chunks:
            table_copy(chunk + AHEAD).start()
        values = jnp.dot(leaf_ref[...], table_ref[chunk], preferred_element_type=jnp.float32)
        real = values[:leaves].reshape(leaves // octants, octants, width)
        imag = values[leaves:].reshape(leaves // octants, octants, width)
        cos, sin = phase(shift_ref[:, chunk * width : (chunk + 1) * width])
        new_real = jnp.sum(real * cos[None] - imag * sin[None], axis=1)
        new_imag = jnp.sum(real * sin[None] + imag * cos[None], axis=1)
        block = jnp.concatenate([new_real, new_imag], axis=0).astype(out_ref.dtype)
        for part in range(width // sector):
            out_ref[chunk * (width // sector) + part] = block[:, part * sector : (part + 1) * sector]


def spread_rows(block, pattern_ref, first, part):
    pieces = block.shape[1] // LANES
    height = 2 * pieces
    for piece in range(pieces):
        lanes = block[:, piece * LANES : (piece + 1) * LANES]
        start = 2 * first * height + 2 * piece
        pattern_ref[pl.ds(start + part, ROWS, stride=2 * height), :] = lanes
        pattern_ref[pl.ds(start + height + 1 - part, ROWS, stride=2 * height), :] = lanes


def index_copies(hbm_refs, index_refs, sems, head):
    entries = index_refs[0].shape[0]
    parts = (pl.ds(0, head), pl.ds(head, entries - head))
    return [
        [
            pltpu.make_async_copy(hbm_refs[which].at[part], index_refs[which].at[part], sems.at[2 * which + number])
            for which in range(2)
        ]
        for number, part in enumerate(parts)
    ]


def translate(index_refs, first_row, end_row, list_width, trans_ref, pattern_ref, same_ref, cross_ref, height):
    source_ref, offset_ref = index_refs

    def rows_at(step, carry):
        for row in (2 * step, 2 * step + 1):
            same = jnp.zeros((height, LANES), jnp.float32)
            cross = jnp.zeros((height, LANES), jnp.float32)
            for entry in range(list_width):
                source = pl.multiple_of(source_ref[row * list_width + entry], height)
                offset = pl.multiple_of(offset_ref[row * list_width + entry], height)
                factor = trans_ref[pl.ds(offset, height), :]
                same += factor * pattern_ref[pl.ds(source, height), :]
                cross += factor * pattern_ref[pl.ds(source + height, height), :]
            place = pl.ds(pl.multiple_of(row * height, height), height)
            same_ref[place, :] = same
            cross_ref[place, :] = cross
        return carry

    lax.fori_loop(first_row // 2, end_row // 2, rows_at, 0)


def gather_rows(same_ref, cross_ref, first, height):
    real, imag = [], []
    for piece in range(height // 2):
        even = pl.ds(first * height + 2 * piece, ROWS, stride=height)
        odd = pl.ds(first * height + 2 * piece + 1, ROWS, stride=height)
        real.append(same_ref[even, :] - same_ref[odd, :])
        imag.append(cross_ref[even, :] + cross_ref[odd, :])
    return jnp.concatenate(real, axis=1), jnp.concatenate(imag, axis=1)


def tables(shift_ref, table_hbm, cos_ref, sin_ref, table_ref, sem):
    table_copy = pltpu.make_async_copy(table_hbm, table_ref, sem)
    table_copy.start()
    cos_ref[...], sin_ref[...] = phase(shift_ref[:, 0, :])
    table_copy.wait()


def place_of(step):
    return lax.axis_index("box") ^ step


def top_up(mid_ref, table_ref, cos_ref, sin_ref, *out_refs):
    tops, double, sector = mid_ref.shape
    octants = cos_ref.shape[0]
    group = mid_ref[...].reshape(tops * double, sector)
    for step, out_ref in enumerate(out_refs):
        width = out_ref.shape[1]
        columns = pl.ds(pl.multiple_of(place_of(step) * width, width), width)
        values = jnp.dot(group, table_ref[0, :, columns], preferred_element_type=jnp.float32)
        values = values.reshape(tops, double, width)
        real, imag = values[:, :octants], values[:, octants:]
        cos, sin = cos_ref[:, columns], sin_ref[:, columns]
        new_real = jnp.sum(real * cos[None] - imag * sin[None], axis=1)
        new_imag = jnp.sum(real * sin[None] + imag * cos[None], axis=1)
        out_ref[...] = jnp.concatenate([new_real, new_imag], axis=0).astype(out_ref.dtype)


def top_translate(list_width, source_hbm, offset_hbm, trans_ref, *rest):
    count = (len(rest) - 6) // 2
    top_refs, out_refs = rest[:count], rest[count : 2 * count]
    pattern_ref, same_ref, cross_ref, *index_refs, sems = rest[2 * count :]
    head = HEAD_ROWS * list_width
    first_copies, later_copies = index_copies((source_hbm, offset_hbm), index_refs, sems, head)
    for copy in first_copies + later_copies:
        copy.start()
    own, width = top_refs[0].shape
    own = own // 2
    height = 2 * width // LANES
    for step, top_ref in enumerate(top_refs):
        rows = top_ref[...].astype(jnp.float32)
        for first in range(0, own, ROWS):
            base = place_of(step) * own + first
            spread_rows(rows[first : first + ROWS], pattern_ref, base, 0)
            spread_rows(rows[own + first : own + first + ROWS], pattern_ref, base, 1)
    for copy in first_copies:
        copy.wait()
    rest = (list_width, trans_ref, pattern_ref, same_ref, cross_ref, height)
    translate(index_refs, 0, HEAD_ROWS, *rest)
    for copy in later_copies:
        copy.wait()
    translate(index_refs, HEAD_ROWS, count * own, *rest)
    for step, out_ref in enumerate(out_refs):
        real, imag = [], []
        for first in range(0, own, ROWS):
            new_real, new_imag = gather_rows(same_ref, cross_ref, place_of(step) * own + first, height)
            real.append(new_real)
            imag.append(new_imag)
        out_ref[...] = jnp.concatenate(real + imag, axis=0).astype(out_ref.dtype)


def mid_translate(list_width, source_hbm, offset_hbm, trans_ref, *rest):
    group_refs = rest[:-7]
    out_ref, pattern_ref, same_ref, cross_ref, *index_refs, sems = rest[-7:]
    head = HEAD_ROWS * list_width
    first_copies, later_copies = index_copies((source_hbm, offset_hbm), index_refs, sems, head)
    for copy in first_copies + later_copies:
        copy.start()
    for step, group_ref in enumerate(group_refs):
        blocks, _, width = group_ref.shape
        height = 2 * width // LANES
        base = place_of(step) * (blocks * ROWS)
        for block in range(blocks):
            rows = group_ref[block].astype(jnp.float32)
            spread_rows(rows[:ROWS], pattern_ref, base + block * ROWS, 0)
            spread_rows(rows[ROWS:], pattern_ref, base + block * ROWS, 1)
    for copy in first_copies:
        copy.wait()
    rest = (list_width, trans_ref, pattern_ref, same_ref, cross_ref, height)
    translate(index_refs, 0, HEAD_ROWS, *rest)
    for copy in later_copies:
        copy.wait()
    translate(index_refs, HEAD_ROWS, out_ref.shape[1], *rest)
    for first in range(0, out_ref.shape[1], ROWS):
        real, imag = gather_rows(same_ref, cross_ref, first, height)
        out_ref[0, first : first + ROWS] = real
        out_ref[1, first : first + ROWS] = imag


def children_of(parents, cos, sin):
    half = parents.shape[0] // 2
    octants, width = cos.shape
    parents = parents.astype(jnp.float32)
    real, imag = parents[:half, None, :], parents[half:, None, :]
    new_real = (real * cos[None] + imag * sin[None]).reshape(half * octants, width)
    new_imag = (imag * cos[None] - real * sin[None]).reshape(half * octants, width)
    return jnp.concatenate([new_real, new_imag], axis=0).astype(jnp.bfloat16)


ADJOINT = (((1,), (1,)), ((), ()))


def top_down(scale, table_ref, cos_ref, sin_ref, far_ref, *rest):
    top_refs, out_ref = rest[:-1], rest[-1]
    total = None
    for step, top_ref in enumerate(top_refs):
        width = top_ref.shape[1]
        columns = pl.ds(pl.multiple_of(place_of(step) * width, width), width)
        children = children_of(top_ref[...], cos_ref[:, columns], sin_ref[:, columns])
        term = lax.dot_general(children, table_ref[0, :, columns], ADJOINT, preferred_element_type=jnp.float32)
        total = term if total is None else total + term
    half = total.shape[0] // 2
    real = far_ref[0] + scale * total[:half]
    imag = far_ref[1] + scale * total[half:]
    owners, rows, _ = out_ref.shape
    rows = rows // 2
    for owner in range(owners):
        place = slice(owner * rows, (owner + 1) * rows)
        out_ref[owner] = jnp.concatenate([real[place], imag[place]], axis=0).astype(out_ref.dtype)


def leaf_down(scale, mid_ref, table_ref, shift_ref, out_ref, total_ref):
    sectors, _, width = mid_ref.shape
    for part in range(sectors):
        columns = slice(part * width, (part + 1) * width)
        cos, sin = phase(shift_ref[:, columns])
        children = children_of(mid_ref[part], cos, sin)
        term = lax.dot_general(table_ref[:, columns], children, ADJOINT, preferred_element_type=jnp.float32)
        if part == 0:
            total_ref[...] = term
        else:
            total_ref[...] += term
    out_ref[...] = total_ref[...].T * scale


def cost(microseconds):
    return pl.CostEstimate(flops=int(microseconds * 1.15e9), bytes_accessed=0, transcendentals=0)


def params(mebibytes):
    return pltpu.CompilerParams(vmem_limit_bytes=mebibytes * 1024 * 1024)


def rows_of(trans):
    _, offsets, width = trans.shape
    pieces = width // LANES
    rows = jnp.transpose(trans.reshape(2, offsets, pieces, LANES), (1, 2, 0, 3))
    return rows.reshape(offsets * pieces * 2, LANES)


def swap(values, axis, step):
    size = lax.axis_size(axis)
    return lax.ppermute(values, axis, [(k, k ^ step) for k in range(size)])


def pass_on(values_ref, after_ref, out_ref):
    out_ref[...] = values_ref[...]


def follow(values, after):
    vmem = pl.BlockSpec(memory_space=pltpu.VMEM)
    return pl.pallas_call(
        pass_on,
        in_specs=[vmem, pl.BlockSpec(memory_space=pl.ANY)],
        out_specs=vmem,
        out_shape=jax.ShapeDtypeStruct(values.shape, values.dtype),
        compiler_params=params(16),
        cost_estimate=cost(0.1),
        name="pass_on",
    )(values, after)


def exchange(shares):
    received = list(shares)
    for step in reversed(range(1, len(shares))):
        received[step] = swap(shares[step], "box", step)
    return received


def on_device(
    leaf_out,
    interp_mid,
    shift_mid,
    trans_mid,
    list_mid,
    offset_mid,
    interp_top,
    shift_top,
    trans_top,
    list_top,
    offset_top,
):
    boxes = lax.axis_size("box")
    dirs = lax.axis_size("dir")
    box_index = lax.axis_index("box")
    octants = shift_mid.shape[0]
    leaves = leaf_out.shape[1]
    leaf_width, mid_width = interp_mid.shape
    own_mids = leaves // octants
    sector = trans_mid.shape[2]
    top_sector = interp_top.shape[2]
    top_width = trans_top.shape[3]
    mids = list_mid.shape[0]
    group_mids = mids // boxes
    tops = list_top.shape[0]
    group_tops = tops // boxes
    vmem = pl.BlockSpec(memory_space=pltpu.VMEM)
    smem = pl.BlockSpec(memory_space=pltpu.SMEM)
    hbm = pl.BlockSpec(memory_space=pl.ANY)
    top_height = 2 * top_width // LANES
    mid_height = 2 * sector // LANES

    chunk = sector * math.gcd(dirs, CHUNK_SECTORS)
    chunks = mid_width // chunk
    outgoing = pl.pallas_call(
        leaf_up,
        in_specs=[hbm, hbm, hbm],
        out_specs=vmem,
        out_shape=jax.ShapeDtypeStruct((dirs, 2 * own_mids, sector), jnp.bfloat16),
        scratch_shapes=[
            pltpu.VMEM((2 * leaves, leaf_width), jnp.bfloat16),
            pltpu.VMEM((octants, mid_width), jnp.float32),
            pltpu.VMEM((chunks, leaf_width, chunk), jnp.bfloat16),
            pltpu.SemaphoreType.DMA((2,)),
            pltpu.SemaphoreType.DMA((chunks,)),
        ],
        compiler_params=params(60),
        cost_estimate=cost(5),
        name="leaf_up",
    )(leaf_out.reshape(2 * leaves, leaf_width), interp_mid, shift_mid)
    mid_own = lax.all_to_all(outgoing, "dir", split_axis=0, concat_axis=0, tiled=True)

    list_width = list_mid.shape[1]
    top_index = [(list_top * (2 * top_height)).reshape(-1), (offset_top * top_height).reshape(-1)]
    own_list = lax.dynamic_slice_in_dim(list_mid, box_index * group_mids, group_mids, 0)
    own_offsets = lax.dynamic_slice_in_dim(offset_mid, box_index * group_mids, group_mids, 0)
    mid_index = [(own_list * (2 * mid_height)).reshape(-1), (own_offsets * mid_height).reshape(-1)]
    rows_top = rows_of(trans_top.reshape(2, -1, top_width))
    rows_mid = rows_of(trans_mid)
    table = jax.ShapeDtypeStruct((octants, top_sector), jnp.float32)
    cos_top, sin_top, table_top = pl.pallas_call(
        tables,
        in_specs=[vmem, hbm],
        out_specs=[vmem] * 3,
        out_shape=[table, table, jax.ShapeDtypeStruct(interp_top.shape, interp_top.dtype)],
        scratch_shapes=[pltpu.SemaphoreType.DMA],
        compiler_params=params(16),
        cost_estimate=cost(2),
        name="tables",
    )(shift_top, interp_top)
    ready = (mid_own, top_index, mid_index, rows_top, cos_top, sin_top, table_top)
    mid_own, top_index, mid_index, rows_top, cos_top, sin_top, table_top = lax.optimization_barrier(ready)

    share = jax.ShapeDtypeStruct((2 * dirs, top_width), jnp.bfloat16)
    top_out = pl.pallas_call(
        top_up,
        in_specs=[vmem] * 4,
        out_specs=[vmem] * boxes,
        out_shape=[share] * boxes,
        compiler_params=params(16),
        cost_estimate=cost(1),
        name="top_up",
    )(mid_own, table_top, cos_top, sin_top)
    top_all = exchange(top_out)

    groups = {0: follow(mid_own, top_out[0])}
    bits = [1 << k for k in reversed(range(boxes.bit_length() - 1))]
    for bit in bits:
        groups[bit] = swap(groups[0], "box", bit)

    top_in = pl.pallas_call(
        functools.partial(top_translate, list_width),
        in_specs=[hbm, hbm, vmem] + [vmem] * boxes,
        out_specs=[vmem] * boxes,
        out_shape=[share] * boxes,
        scratch_shapes=[
            pltpu.VMEM((2 * tops * top_height, LANES), jnp.float32),
            pltpu.VMEM((tops * top_height, LANES), jnp.float32),
            pltpu.VMEM((tops * top_height, LANES), jnp.float32),
            pltpu.SMEM(top_index[0].shape, jnp.int32),
            pltpu.SMEM(top_index[0].shape, jnp.int32),
            pltpu.SemaphoreType.DMA((4,)),
        ],
        compiler_params=params(16),
        cost_estimate=cost(15),
        name="top_translate",
    )(*top_index, rows_top, *top_all)
    top_back = exchange(top_in)

    for number, bit in enumerate(bits[1:], 1):
        for step in [step for step in groups if step and not step & (2 * bit - 1)]:
            values = follow(groups[step], top_in[0]) if number == 1 else groups[step]
            groups[step ^ bit] = swap(values, "box", bit)

    mid_far = pl.pallas_call(
        functools.partial(mid_translate, list_width),
        in_specs=[hbm, hbm, vmem] + [vmem] * boxes,
        out_specs=vmem,
        out_shape=jax.ShapeDtypeStruct((2, group_mids, sector), jnp.float32),
        scratch_shapes=[
            pltpu.VMEM((2 * mids * mid_height, LANES), jnp.float32),
            pltpu.VMEM((group_mids * mid_height, LANES), jnp.float32),
            pltpu.VMEM((group_mids * mid_height, LANES), jnp.float32),
            pltpu.SMEM(mid_index[0].shape, jnp.int32),
            pltpu.SMEM(mid_index[0].shape, jnp.int32),
            pltpu.SemaphoreType.DMA((4,)),
        ],
        compiler_params=params(16),
        cost_estimate=cost(1),
        name="mid_translate",
    )(*mid_index, rows_mid, *[groups[step] for step in range(boxes)])

    incoming = pl.pallas_call(
        functools.partial(top_down, sector / top_sector),
        in_specs=[vmem] * (4 + boxes),
        out_specs=vmem,
        out_shape=jax.ShapeDtypeStruct((dirs, 2 * own_mids, sector), jnp.bfloat16),
        compiler_params=params(16),
        cost_estimate=cost(1),
        name="top_down",
    )(table_top, cos_top, sin_top, mid_far, *top_back)
    mid_back = lax.all_to_all(incoming, "dir", split_axis=0, concat_axis=0, tiled=True)

    leaf_in = pl.pallas_call(
        functools.partial(leaf_down, leaf_width / mid_width),
        in_specs=[vmem] * 3,
        out_specs=vmem,
        out_shape=jax.ShapeDtypeStruct((2 * leaves, leaf_width), jnp.float32),
        scratch_shapes=[pltpu.VMEM((leaf_width, 2 * leaves), jnp.float32)],
        compiler_params=params(20),
        cost_estimate=cost(3),
        name="leaf_down",
    )(mid_back, interp_mid, shift_mid)
    return leaf_in.reshape(2, leaves, leaf_width)


def solution(mesh):
    return jax.shard_map(
        on_device,
        mesh=mesh,
        in_specs=(
            P(None, ("box", "dir"), None),
            P(),
            P(),
            P(None, None, "dir"),
            P(),
            P(),
            P("dir", None, None),
            P(None, "dir", None),
            P(None, None, "dir", "box"),
            P(),
            P(),
        ),
        out_specs=P(None, ("box", "dir"), None),
        check_vma=False,
    )
```

```python
import functools
import math

import jax
import jax.numpy as jnp
from jax import lax
from jax.experimental import pallas as pl
from jax.experimental.pallas import tpu as pltpu
from jax.sharding import PartitionSpec as P

SINE = (1.0, -0.16666647791862488, 0.00833289884030819, -0.0001980085507966578, 2.5904087124217767e-06)
COSINE = (1.0, -0.5, 0.04166663438081741, -0.0013888360699638724, 2.476012559782248e-05, -2.6050881274386484e-07)
HEAD_ROWS = 4
UNROLL = 4
LANES = 128
ROWS = 8
AHEAD = 2
CHUNK_SECTORS = 2


def powers(square, factors):
    total = jnp.full_like(square, factors[-1])
    for factor in factors[-2::-1]:
        total = total * square + factor
    return total


def phase(angle):
    half = angle * 0.5
    square = half * half
    sine = half * powers(square, SINE)
    cosine = powers(square, COSINE)
    return 1.0 - 2.0 * sine * sine, 2.0 * sine * cosine


def leaf_up(leaf_hbm, table_hbm, shift_hbm, out_ref, leaf_ref, shift_ref, table_ref, small_sems, table_sems):
    chunks, _, width = table_ref.shape
    octants = shift_ref.shape[0]
    sector = out_ref.shape[2]
    leaf_copy = pltpu.make_async_copy(leaf_hbm, leaf_ref, small_sems.at[0])
    shift_copy = pltpu.make_async_copy(shift_hbm, shift_ref, small_sems.at[1])

    def table_copy(chunk):
        source = table_hbm.at[:, pl.ds(chunk * width, width)]
        return pltpu.make_async_copy(source, table_ref.at[chunk], table_sems.at[chunk])

    leaf_copy.start()
    table_copy(0).start()
    shift_copy.start()
    for chunk in range(1, min(AHEAD, chunks)):
        table_copy(chunk).start()
    leaf_copy.wait()
    shift_copy.wait()
    leaves = leaf_ref.shape[0] // 2
    for chunk in range(chunks):
        table_copy(chunk).wait()
        if chunk + AHEAD < chunks:
            table_copy(chunk + AHEAD).start()
        values = jnp.dot(leaf_ref[...], table_ref[chunk], preferred_element_type=jnp.float32)
        real = values[:leaves].reshape(leaves // octants, octants, width)
        imag = values[leaves:].reshape(leaves // octants, octants, width)
        cos, sin = phase(shift_ref[:, chunk * width : (chunk + 1) * width])
        new_real = jnp.sum(real * cos[None] - imag * sin[None], axis=1)
        new_imag = jnp.sum(real * sin[None] + imag * cos[None], axis=1)
        block = jnp.concatenate([new_real, new_imag], axis=0).astype(out_ref.dtype)
        for part in range(width // sector):
            out_ref[chunk * (width // sector) + part] = block[:, part * sector : (part + 1) * sector]


def spread_rows(block, pattern_ref, first, part):
    pieces = block.shape[1] // LANES
    height = 2 * pieces
    for piece in range(pieces):
        lanes = block[:, piece * LANES : (piece + 1) * LANES]
        start = 2 * first * height + 2 * piece
        pattern_ref[pl.ds(start + part, ROWS, stride=2 * height), :] = lanes
        pattern_ref[pl.ds(start + height + 1 - part, ROWS, stride=2 * height), :] = lanes


def index_copies(hbm_refs, index_refs, sems, head):
    entries = index_refs[0].shape[0]
    parts = (pl.ds(0, head), pl.ds(head, entries - head))
    return [
        [
            pltpu.make_async_copy(hbm_refs[which].at[part], index_refs[which].at[part], sems.at[2 * which + number])
            for which in range(2)
        ]
        for number, part in enumerate(parts)
    ]


def translate(index_refs, first_row, end_row, list_width, trans_ref, pattern_ref, same_ref, cross_ref, height):
    source_ref, offset_ref = index_refs

    def rows_at(step, carry):
        for row in [UNROLL * step + k for k in range(UNROLL)]:
            same = jnp.zeros((height, LANES), jnp.float32)
            cross = jnp.zeros((height, LANES), jnp.float32)
            for entry in range(list_width):
                source = pl.multiple_of(source_ref[row * list_width + entry], height)
                offset = pl.multiple_of(offset_ref[row * list_width + entry], height)
                factor = trans_ref[pl.ds(offset, height), :]
                same += factor * pattern_ref[pl.ds(source, height), :]
                cross += factor * pattern_ref[pl.ds(source + height, height), :]
            place = pl.ds(pl.multiple_of(row * height, height), height)
            same_ref[place, :] = same
            cross_ref[place, :] = cross
        return carry

    lax.fori_loop(first_row // UNROLL, end_row // UNROLL, rows_at, 0)


def gather_rows(same_ref, cross_ref, first, height):
    real, imag = [], []
    for piece in range(height // 2):
        even = pl.ds(first * height + 2 * piece, ROWS, stride=height)
        odd = pl.ds(first * height + 2 * piece + 1, ROWS, stride=height)
        real.append(same_ref[even, :] - same_ref[odd, :])
        imag.append(cross_ref[even, :] + cross_ref[odd, :])
    return jnp.concatenate(real, axis=1), jnp.concatenate(imag, axis=1)


def tables(shift_ref, cos_ref, sin_ref):
    cos_ref[...], sin_ref[...] = phase(shift_ref[:, 0, :])


def place_of(step):
    return lax.axis_index("box") ^ step


def top_up(mid_ref, table_ref, cos_ref, sin_ref, *out_refs):
    tops, double, sector = mid_ref.shape
    octants = cos_ref.shape[0]
    group = mid_ref[...].reshape(tops * double, sector)
    for step, out_ref in enumerate(out_refs):
        width = out_ref.shape[1]
        columns = pl.ds(pl.multiple_of(place_of(step) * width, width), width)
        values = jnp.dot(group, table_ref[0, :, columns], preferred_element_type=jnp.float32)
        values = values.reshape(tops, double, width)
        real, imag = values[:, :octants], values[:, octants:]
        cos, sin = cos_ref[:, columns], sin_ref[:, columns]
        new_real = jnp.sum(real * cos[None] - imag * sin[None], axis=1)
        new_imag = jnp.sum(real * sin[None] + imag * cos[None], axis=1)
        out_ref[...] = jnp.concatenate([new_real, new_imag], axis=0).astype(out_ref.dtype)


def top_translate(list_width, source_hbm, offset_hbm, plane_ref, *rest):
    count = (len(rest) - 7) // 2
    top_refs, out_refs = rest[:count], rest[count : 2 * count]
    trans_ref, pattern_ref, same_ref, cross_ref, *index_refs, sems = rest[2 * count :]
    head = HEAD_ROWS * list_width
    first_copies, later_copies = index_copies((source_hbm, offset_hbm), index_refs, sems, head)
    for copy in first_copies + later_copies:
        copy.start()
    plane = plane_ref.shape[0] // 2
    for part in range(2):
        trans_ref[pl.ds(part, plane, stride=2), :] = plane_ref[part * plane : (part + 1) * plane, :]
    own, width = top_refs[0].shape
    own = own // 2
    height = 2 * width // LANES
    for step, top_ref in enumerate(top_refs):
        rows = top_ref[...].astype(jnp.float32)
        for first in range(0, own, ROWS):
            base = place_of(step) * own + first
            spread_rows(rows[first : first + ROWS], pattern_ref, base, 0)
            spread_rows(rows[own + first : own + first + ROWS], pattern_ref, base, 1)
    for copy in first_copies:
        copy.wait()
    rest = (list_width, trans_ref, pattern_ref, same_ref, cross_ref, height)
    translate(index_refs, 0, HEAD_ROWS, *rest)
    for copy in later_copies:
        copy.wait()
    translate(index_refs, HEAD_ROWS, count * own, *rest)
    for step, out_ref in enumerate(out_refs):
        real, imag = [], []
        for first in range(0, own, ROWS):
            new_real, new_imag = gather_rows(same_ref, cross_ref, place_of(step) * own + first, height)
            real.append(new_real)
            imag.append(new_imag)
        out_ref[...] = jnp.concatenate(real + imag, axis=0).astype(out_ref.dtype)


def mid_translate(list_width, source_hbm, offset_hbm, trans_ref, *rest):
    group_refs = rest[:-7]
    out_ref, pattern_ref, same_ref, cross_ref, *index_refs, sems = rest[-7:]
    head = HEAD_ROWS * list_width
    first_copies, later_copies = index_copies((source_hbm, offset_hbm), index_refs, sems, head)
    for copy in first_copies + later_copies:
        copy.start()
    for step, group_ref in enumerate(group_refs):
        blocks, _, width = group_ref.shape
        height = 2 * width // LANES
        base = place_of(step) * (blocks * ROWS)
        for block in range(blocks):
            rows = group_ref[block].astype(jnp.float32)
            spread_rows(rows[:ROWS], pattern_ref, base + block * ROWS, 0)
            spread_rows(rows[ROWS:], pattern_ref, base + block * ROWS, 1)
    for copy in first_copies:
        copy.wait()
    rest = (list_width, trans_ref, pattern_ref, same_ref, cross_ref, height)
    translate(index_refs, 0, HEAD_ROWS, *rest)
    for copy in later_copies:
        copy.wait()
    translate(index_refs, HEAD_ROWS, out_ref.shape[1], *rest)
    for first in range(0, out_ref.shape[1], ROWS):
        real, imag = gather_rows(same_ref, cross_ref, first, height)
        out_ref[0, first : first + ROWS] = real
        out_ref[1, first : first + ROWS] = imag


def children_of(parents, cos, sin):
    half = parents.shape[0] // 2
    octants, width = cos.shape
    parents = parents.astype(jnp.float32)
    real, imag = parents[:half, None, :], parents[half:, None, :]
    new_real = (real * cos[None] + imag * sin[None]).reshape(half * octants, width)
    new_imag = (imag * cos[None] - real * sin[None]).reshape(half * octants, width)
    return jnp.concatenate([new_real, new_imag], axis=0).astype(jnp.bfloat16)


ADJOINT = (((1,), (1,)), ((), ()))


def top_down(scale, table_ref, cos_ref, sin_ref, far_ref, *rest):
    top_refs, out_ref = rest[:-1], rest[-1]
    total = None
    for step, top_ref in enumerate(top_refs):
        width = top_ref.shape[1]
        columns = pl.ds(pl.multiple_of(place_of(step) * width, width), width)
        children = children_of(top_ref[...], cos_ref[:, columns], sin_ref[:, columns])
        term = lax.dot_general(children, table_ref[0, :, columns], ADJOINT, preferred_element_type=jnp.float32)
        total = term if total is None else total + term
    half = total.shape[0] // 2
    real = far_ref[0] + scale * total[:half]
    imag = far_ref[1] + scale * total[half:]
    owners, rows, _ = out_ref.shape
    rows = rows // 2
    for owner in range(owners):
        place = slice(owner * rows, (owner + 1) * rows)
        out_ref[owner] = jnp.concatenate([real[place], imag[place]], axis=0).astype(out_ref.dtype)


def leaf_down(scale, mid_ref, table_ref, shift_ref, out_ref, total_ref):
    sectors, _, width = mid_ref.shape
    for part in range(sectors):
        columns = slice(part * width, (part + 1) * width)
        cos, sin = phase(shift_ref[:, columns])
        children = children_of(mid_ref[part], cos, sin)
        term = lax.dot_general(table_ref[:, columns], children, ADJOINT, preferred_element_type=jnp.float32)
        if part == 0:
            total_ref[...] = term
        else:
            total_ref[...] += term
    out_ref[...] = total_ref[...].T * scale


def cost(microseconds):
    return pl.CostEstimate(flops=int(microseconds * 1.15e9), bytes_accessed=0, transcendentals=0)


def params(mebibytes):
    return pltpu.CompilerParams(vmem_limit_bytes=mebibytes * 1024 * 1024)


def rows_of(trans):
    _, offsets, width = trans.shape
    pieces = width // LANES
    rows = jnp.transpose(trans.reshape(2, offsets, pieces, LANES), (1, 2, 0, 3))
    return rows.reshape(offsets * pieces * 2, LANES)


def swap(values, axis, step):
    size = lax.axis_size(axis)
    return lax.ppermute(values, axis, [(k, k ^ step) for k in range(size)])


def pass_on(values_ref, after_ref, out_ref):
    out_ref[...] = values_ref[...]


def follow(values, after):
    vmem = pl.BlockSpec(memory_space=pltpu.VMEM)
    return pl.pallas_call(
        pass_on,
        in_specs=[vmem, pl.BlockSpec(memory_space=pl.ANY)],
        out_specs=vmem,
        out_shape=jax.ShapeDtypeStruct(values.shape, values.dtype),
        compiler_params=params(16),
        cost_estimate=cost(0.1),
        name="pass_on",
    )(values, after)


def exchange(shares):
    received = list(shares)
    for step in reversed(range(1, len(shares))):
        received[step] = swap(shares[step], "box", step)
    return received


def on_device(
    leaf_out,
    interp_mid,
    shift_mid,
    trans_mid,
    list_mid,
    offset_mid,
    interp_top,
    shift_top,
    trans_top,
    list_top,
    offset_top,
):
    boxes = lax.axis_size("box")
    dirs = lax.axis_size("dir")
    box_index = lax.axis_index("box")
    octants = shift_mid.shape[0]
    leaves = leaf_out.shape[1]
    leaf_width, mid_width = interp_mid.shape
    own_mids = leaves // octants
    sector = trans_mid.shape[2]
    top_sector = interp_top.shape[2]
    top_width = trans_top.shape[3]
    mids = list_mid.shape[0]
    group_mids = mids // boxes
    tops = list_top.shape[0]
    group_tops = tops // boxes
    vmem = pl.BlockSpec(memory_space=pltpu.VMEM)
    smem = pl.BlockSpec(memory_space=pltpu.SMEM)
    hbm = pl.BlockSpec(memory_space=pl.ANY)
    top_height = 2 * top_width // LANES
    mid_height = 2 * sector // LANES

    chunk = sector * math.gcd(dirs, CHUNK_SECTORS)
    chunks = mid_width // chunk
    outgoing = pl.pallas_call(
        leaf_up,
        in_specs=[hbm, hbm, hbm],
        out_specs=vmem,
        out_shape=jax.ShapeDtypeStruct((dirs, 2 * own_mids, sector), jnp.bfloat16),
        scratch_shapes=[
            pltpu.VMEM((2 * leaves, leaf_width), jnp.bfloat16),
            pltpu.VMEM((octants, mid_width), jnp.float32),
            pltpu.VMEM((chunks, leaf_width, chunk), jnp.bfloat16),
            pltpu.SemaphoreType.DMA((2,)),
            pltpu.SemaphoreType.DMA((chunks,)),
        ],
        compiler_params=params(60),
        cost_estimate=cost(5),
        name="leaf_up",
    )(leaf_out.reshape(2 * leaves, leaf_width), interp_mid, shift_mid)
    mid_own = lax.all_to_all(outgoing, "dir", split_axis=0, concat_axis=0, tiled=True)

    list_width = list_mid.shape[1]
    top_index = [(list_top * (2 * top_height)).reshape(-1), (offset_top * top_height).reshape(-1)]
    own_list = lax.dynamic_slice_in_dim(list_mid, box_index * group_mids, group_mids, 0)
    own_offsets = lax.dynamic_slice_in_dim(offset_mid, box_index * group_mids, group_mids, 0)
    mid_index = [(own_list * (2 * mid_height)).reshape(-1), (own_offsets * mid_height).reshape(-1)]
    rows_top = trans_top.reshape(-1, LANES)
    rows_mid = rows_of(trans_mid)
    table = jax.ShapeDtypeStruct((octants, top_sector), jnp.float32)
    cos_top, sin_top = pl.pallas_call(
        tables,
        in_specs=[vmem],
        out_specs=[vmem] * 2,
        out_shape=[table, table],
        compiler_params=params(16),
        cost_estimate=cost(2),
        name="tables",
    )(shift_top)
    ready = (mid_own, top_index, mid_index, cos_top, sin_top)
    mid_own, top_index, mid_index, cos_top, sin_top = lax.optimization_barrier(ready)

    share = jax.ShapeDtypeStruct((2 * dirs, top_width), jnp.bfloat16)
    top_out = pl.pallas_call(
        top_up,
        in_specs=[vmem] * 4,
        out_specs=[vmem] * boxes,
        out_shape=[share] * boxes,
        compiler_params=params(16),
        cost_estimate=cost(4),
        name="top_up",
    )(mid_own, interp_top, cos_top, sin_top)
    top_all = exchange(top_out)

    groups = {0: follow(mid_own, top_out[0])}
    bits = [1 << k for k in reversed(range(boxes.bit_length() - 1))]
    for bit in bits:
        groups[bit] = swap(groups[0], "box", bit)

    top_in = pl.pallas_call(
        functools.partial(top_translate, list_width),
        in_specs=[hbm, hbm, vmem] + [vmem] * boxes,
        out_specs=[vmem] * boxes,
        out_shape=[share] * boxes,
        scratch_shapes=[
            pltpu.VMEM(rows_top.shape, jnp.float32),
            pltpu.VMEM((2 * tops * top_height, LANES), jnp.float32),
            pltpu.VMEM((tops * top_height, LANES), jnp.float32),
            pltpu.VMEM((tops * top_height, LANES), jnp.float32),
            pltpu.SMEM(top_index[0].shape, jnp.int32),
            pltpu.SMEM(top_index[0].shape, jnp.int32),
            pltpu.SemaphoreType.DMA((4,)),
        ],
        compiler_params=params(16),
        cost_estimate=cost(15),
        name="top_translate",
    )(*top_index, rows_top, *top_all)
    top_back = exchange(top_in)

    for number, bit in enumerate(bits[1:], 1):
        for step in [step for step in groups if step and not step & (2 * bit - 1)]:
            values = follow(groups[step], top_in[0]) if number == 1 else groups[step]
            groups[step ^ bit] = swap(values, "box", bit)

    mid_far = pl.pallas_call(
        functools.partial(mid_translate, list_width),
        in_specs=[hbm, hbm, vmem] + [vmem] * boxes,
        out_specs=vmem,
        out_shape=jax.ShapeDtypeStruct((2, group_mids, sector), jnp.float32),
        scratch_shapes=[
            pltpu.VMEM((2 * mids * mid_height, LANES), jnp.float32),
            pltpu.VMEM((group_mids * mid_height, LANES), jnp.float32),
            pltpu.VMEM((group_mids * mid_height, LANES), jnp.float32),
            pltpu.SMEM(mid_index[0].shape, jnp.int32),
            pltpu.SMEM(mid_index[0].shape, jnp.int32),
            pltpu.SemaphoreType.DMA((4,)),
        ],
        compiler_params=params(16),
        cost_estimate=cost(1),
        name="mid_translate",
    )(*mid_index, rows_mid, *[groups[step] for step in range(boxes)])

    incoming = pl.pallas_call(
        functools.partial(top_down, sector / top_sector),
        in_specs=[vmem] * (4 + boxes),
        out_specs=vmem,
        out_shape=jax.ShapeDtypeStruct((dirs, 2 * own_mids, sector), jnp.bfloat16),
        compiler_params=params(16),
        cost_estimate=cost(1),
        name="top_down",
    )(interp_top, cos_top, sin_top, mid_far, *top_back)
    mid_back = lax.all_to_all(incoming, "dir", split_axis=0, concat_axis=0, tiled=True)

    leaf_in = pl.pallas_call(
        functools.partial(leaf_down, leaf_width / mid_width),
        in_specs=[vmem] * 3,
        out_specs=vmem,
        out_shape=jax.ShapeDtypeStruct((2 * leaves, leaf_width), jnp.float32),
        scratch_shapes=[pltpu.VMEM((leaf_width, 2 * leaves), jnp.float32)],
        compiler_params=params(20),
        cost_estimate=cost(3),
        name="leaf_down",
    )(mid_back, interp_mid, shift_mid)
    return leaf_in.reshape(2, leaves, leaf_width)


def solution(mesh):
    return jax.shard_map(
        on_device,
        mesh=mesh,
        in_specs=(
            P(None, ("box", "dir"), None),
            P(),
            P(),
            P(None, None, "dir"),
            P(),
            P(),
            P("dir", None, None),
            P(None, "dir", None),
            P(None, None, "dir", "box"),
            P(),
            P(),
        ),
        out_specs=P(None, ("box", "dir"), None),
        check_vma=False,
    )
```

```python
import functools
import math

import jax
import jax.numpy as jnp
from jax import lax
from jax.experimental import pallas as pl
from jax.experimental.pallas import tpu as pltpu
from jax.sharding import PartitionSpec as P

SINE = (1.0, -0.16666647791862488, 0.00833289884030819, -0.0001980085507966578, 2.5904087124217767e-06)
COSINE = (1.0, -0.5, 0.04166663438081741, -0.0013888360699638724, 2.476012559782248e-05, -2.6050881274386484e-07)
HEAD_ROWS = 4
UNROLL = 4
LANES = 128
ROWS = 8
AHEAD = 3
CHUNK_SECTORS = 2


def powers(square, factors):
    total = jnp.full_like(square, factors[-1])
    for factor in factors[-2::-1]:
        total = total * square + factor
    return total


def phase(angle):
    half = angle * 0.5
    square = half * half
    sine = half * powers(square, SINE)
    cosine = powers(square, COSINE)
    return 1.0 - 2.0 * sine * sine, 2.0 * sine * cosine


def leaf_up(leaf_hbm, table_hbm, shift_hbm, out_ref, leaf_ref, shift_ref, table_ref, small_sems, table_sems):
    chunks, _, width = table_ref.shape
    octants = shift_ref.shape[0]
    sector = out_ref.shape[2]
    leaf_copy = pltpu.make_async_copy(leaf_hbm, leaf_ref, small_sems.at[0])
    shift_copy = pltpu.make_async_copy(shift_hbm, shift_ref, small_sems.at[1])

    def table_copy(chunk):
        source = table_hbm.at[:, pl.ds(chunk * width, width)]
        return pltpu.make_async_copy(source, table_ref.at[chunk], table_sems.at[chunk])

    leaf_copy.start()
    table_copy(0).start()
    shift_copy.start()
    for chunk in range(1, min(AHEAD, chunks)):
        table_copy(chunk).start()
    leaf_copy.wait()
    shift_copy.wait()
    leaves = leaf_ref.shape[0] // 2
    for chunk in range(chunks):
        table_copy(chunk).wait()
        if chunk + AHEAD < chunks:
            table_copy(chunk + AHEAD).start()
        values = jnp.dot(leaf_ref[...], table_ref[chunk], preferred_element_type=jnp.float32)
        real = values[:leaves].reshape(leaves // octants, octants, width)
        imag = values[leaves:].reshape(leaves // octants, octants, width)
        cos, sin = phase(shift_ref[:, chunk * width : (chunk + 1) * width])
        new_real = jnp.sum(real * cos[None] - imag * sin[None], axis=1)
        new_imag = jnp.sum(real * sin[None] + imag * cos[None], axis=1)
        block = jnp.concatenate([new_real, new_imag], axis=0).astype(out_ref.dtype)
        for part in range(width // sector):
            out_ref[chunk * (width // sector) + part] = block[:, part * sector : (part + 1) * sector]


def spread_rows(block, pattern_ref, first, part):
    pieces = block.shape[1] // LANES
    height = 2 * pieces
    for piece in range(pieces):
        lanes = block[:, piece * LANES : (piece + 1) * LANES]
        start = 2 * first * height + 2 * piece
        pattern_ref[pl.ds(start + part, ROWS, stride=2 * height), :] = lanes
        pattern_ref[pl.ds(start + height + 1 - part, ROWS, stride=2 * height), :] = lanes


def index_copies(hbm_refs, index_refs, sems, head):
    entries = index_refs[0].shape[0]
    parts = (pl.ds(0, head), pl.ds(head, entries - head))
    return [
        [
            pltpu.make_async_copy(hbm_refs[which].at[part], index_refs[which].at[part], sems.at[2 * which + number])
            for which in range(2)
        ]
        for number, part in enumerate(parts)
    ]


def translate(index_refs, first_row, end_row, list_width, trans_ref, pattern_ref, same_ref, cross_ref, height):
    source_ref, offset_ref = index_refs

    def rows_at(step, carry):
        for row in [UNROLL * step + k for k in range(UNROLL)]:
            same = jnp.zeros((height, LANES), jnp.float32)
            cross = jnp.zeros((height, LANES), jnp.float32)
            for entry in range(list_width):
                source = pl.multiple_of(source_ref[row * list_width + entry], height)
                offset = pl.multiple_of(offset_ref[row * list_width + entry], height)
                factor = trans_ref[pl.ds(offset, height), :]
                same += factor * pattern_ref[pl.ds(source, height), :]
                cross += factor * pattern_ref[pl.ds(source + height, height), :]
            place = pl.ds(pl.multiple_of(row * height, height), height)
            same_ref[place, :] = same
            cross_ref[place, :] = cross
        return carry

    lax.fori_loop(first_row // UNROLL, end_row // UNROLL, rows_at, 0)


def gather_rows(same_ref, cross_ref, first, height):
    real, imag = [], []
    for piece in range(height // 2):
        even = pl.ds(first * height + 2 * piece, ROWS, stride=height)
        odd = pl.ds(first * height + 2 * piece + 1, ROWS, stride=height)
        real.append(same_ref[even, :] - same_ref[odd, :])
        imag.append(cross_ref[even, :] + cross_ref[odd, :])
    return jnp.concatenate(real, axis=1), jnp.concatenate(imag, axis=1)


def tables(shift_ref, cos_ref, sin_ref):
    cos_ref[...], sin_ref[...] = phase(shift_ref[:, 0, :])


def place_of(step):
    return lax.axis_index("box") ^ step


def top_up(mid_ref, table_ref, cos_ref, sin_ref, *out_refs):
    tops, double, sector = mid_ref.shape
    octants = cos_ref.shape[0]
    group = mid_ref[...].reshape(tops * double, sector)
    for step, out_ref in enumerate(out_refs):
        width = out_ref.shape[1]
        columns = pl.ds(pl.multiple_of(place_of(step) * width, width), width)
        values = jnp.dot(group, table_ref[0, :, columns], preferred_element_type=jnp.float32)
        values = values.reshape(tops, double, width)
        real, imag = values[:, :octants], values[:, octants:]
        cos, sin = cos_ref[:, columns], sin_ref[:, columns]
        new_real = jnp.sum(real * cos[None] - imag * sin[None], axis=1)
        new_imag = jnp.sum(real * sin[None] + imag * cos[None], axis=1)
        out_ref[...] = jnp.concatenate([new_real, new_imag], axis=0).astype(out_ref.dtype)


def top_translate(list_width, source_hbm, offset_hbm, plane_ref, *rest):
    count = (len(rest) - 7) // 2
    top_refs, out_refs = rest[:count], rest[count : 2 * count]
    trans_ref, pattern_ref, same_ref, cross_ref, *index_refs, sems = rest[2 * count :]
    head = HEAD_ROWS * list_width
    first_copies, later_copies = index_copies((source_hbm, offset_hbm), index_refs, sems, head)
    for copy in first_copies + later_copies:
        copy.start()
    plane = plane_ref.shape[0] // 2
    for part in range(2):
        trans_ref[pl.ds(part, plane, stride=2), :] = plane_ref[part * plane : (part + 1) * plane, :]
    own, width = top_refs[0].shape
    own = own // 2
    height = 2 * width // LANES
    for step, top_ref in enumerate(top_refs):
        rows = top_ref[...].astype(jnp.float32)
        for first in range(0, own, ROWS):
            base = place_of(step) * own + first
            spread_rows(rows[first : first + ROWS], pattern_ref, base, 0)
            spread_rows(rows[own + first : own + first + ROWS], pattern_ref, base, 1)
    for copy in first_copies:
        copy.wait()
    rest = (list_width, trans_ref, pattern_ref, same_ref, cross_ref, height)
    translate(index_refs, 0, HEAD_ROWS, *rest)
    for copy in later_copies:
        copy.wait()
    translate(index_refs, HEAD_ROWS, count * own, *rest)
    for step, out_ref in enumerate(out_refs):
        real, imag = [], []
        for first in range(0, own, ROWS):
            new_real, new_imag = gather_rows(same_ref, cross_ref, place_of(step) * own + first, height)
            real.append(new_real)
            imag.append(new_imag)
        out_ref[...] = jnp.concatenate(real + imag, axis=0).astype(out_ref.dtype)


def mid_translate(list_width, source_hbm, offset_hbm, trans_ref, *rest):
    group_refs = rest[:-7]
    out_ref, pattern_ref, same_ref, cross_ref, *index_refs, sems = rest[-7:]
    head = HEAD_ROWS * list_width
    first_copies, later_copies = index_copies((source_hbm, offset_hbm), index_refs, sems, head)
    for copy in first_copies + later_copies:
        copy.start()
    for step, group_ref in enumerate(group_refs):
        blocks, _, width = group_ref.shape
        height = 2 * width // LANES
        base = place_of(step) * (blocks * ROWS)
        for block in range(blocks):
            rows = group_ref[block].astype(jnp.float32)
            spread_rows(rows[:ROWS], pattern_ref, base + block * ROWS, 0)
            spread_rows(rows[ROWS:], pattern_ref, base + block * ROWS, 1)
    for copy in first_copies:
        copy.wait()
    rest = (list_width, trans_ref, pattern_ref, same_ref, cross_ref, height)
    translate(index_refs, 0, HEAD_ROWS, *rest)
    for copy in later_copies:
        copy.wait()
    translate(index_refs, HEAD_ROWS, out_ref.shape[1], *rest)
    for first in range(0, out_ref.shape[1], ROWS):
        real, imag = gather_rows(same_ref, cross_ref, first, height)
        out_ref[0, first : first + ROWS] = real
        out_ref[1, first : first + ROWS] = imag


def children_of(parents, cos, sin):
    half = parents.shape[0] // 2
    octants, width = cos.shape
    parents = parents.astype(jnp.float32)
    real, imag = parents[:half, None, :], parents[half:, None, :]
    new_real = (real * cos[None] + imag * sin[None]).reshape(half * octants, width)
    new_imag = (imag * cos[None] - real * sin[None]).reshape(half * octants, width)
    return jnp.concatenate([new_real, new_imag], axis=0).astype(jnp.bfloat16)


ADJOINT = (((1,), (1,)), ((), ()))


def top_down(scale, table_ref, cos_ref, sin_ref, far_ref, *rest):
    top_refs, out_ref = rest[:-1], rest[-1]
    total = None
    for step, top_ref in enumerate(top_refs):
        width = top_ref.shape[1]
        columns = pl.ds(pl.multiple_of(place_of(step) * width, width), width)
        children = children_of(top_ref[...], cos_ref[:, columns], sin_ref[:, columns])
        term = lax.dot_general(children, table_ref[0, :, columns], ADJOINT, preferred_element_type=jnp.float32)
        total = term if total is None else total + term
    half = total.shape[0] // 2
    real = far_ref[0] + scale * total[:half]
    imag = far_ref[1] + scale * total[half:]
    owners, rows, _ = out_ref.shape
    rows = rows // 2
    for owner in range(owners):
        place = slice(owner * rows, (owner + 1) * rows)
        out_ref[owner] = jnp.concatenate([real[place], imag[place]], axis=0).astype(out_ref.dtype)


def leaf_down(scale, mid_ref, table_ref, shift_ref, out_ref, total_ref):
    sectors, _, width = mid_ref.shape
    for part in range(sectors):
        columns = slice(part * width, (part + 1) * width)
        cos, sin = phase(shift_ref[:, columns])
        children = children_of(mid_ref[part], cos, sin)
        term = lax.dot_general(table_ref[:, columns], children, ADJOINT, preferred_element_type=jnp.float32)
        if part == 0:
            total_ref[...] = term
        else:
            total_ref[...] += term
    out_ref[...] = total_ref[...].T * scale


def cost(microseconds):
    return pl.CostEstimate(flops=int(microseconds * 1.15e9), bytes_accessed=0, transcendentals=0)


def params(mebibytes):
    return pltpu.CompilerParams(vmem_limit_bytes=mebibytes * 1024 * 1024)


def rows_of(trans):
    _, offsets, width = trans.shape
    pieces = width // LANES
    rows = jnp.transpose(trans.reshape(2, offsets, pieces, LANES), (1, 2, 0, 3))
    return rows.reshape(offsets * pieces * 2, LANES)


def swap(values, axis, step):
    size = lax.axis_size(axis)
    return lax.ppermute(values, axis, [(k, k ^ step) for k in range(size)])


def pass_on(values_ref, after_ref, out_ref):
    out_ref[...] = values_ref[...]


def follow(values, after):
    vmem = pl.BlockSpec(memory_space=pltpu.VMEM)
    return pl.pallas_call(
        pass_on,
        in_specs=[vmem, pl.BlockSpec(memory_space=pl.ANY)],
        out_specs=vmem,
        out_shape=jax.ShapeDtypeStruct(values.shape, values.dtype),
        compiler_params=params(16),
        cost_estimate=cost(0.1),
        name="pass_on",
    )(values, after)


def exchange(shares):
    received = list(shares)
    for step in range(1, len(shares)):
        received[step] = swap(shares[step], "box", step)
    return received


def on_device(
    leaf_out,
    interp_mid,
    shift_mid,
    trans_mid,
    list_mid,
    offset_mid,
    interp_top,
    shift_top,
    trans_top,
    list_top,
    offset_top,
):
    boxes = lax.axis_size("box")
    dirs = lax.axis_size("dir")
    box_index = lax.axis_index("box")
    octants = shift_mid.shape[0]
    leaves = leaf_out.shape[1]
    leaf_width, mid_width = interp_mid.shape
    own_mids = leaves // octants
    sector = trans_mid.shape[2]
    top_sector = interp_top.shape[2]
    top_width = trans_top.shape[3]
    mids = list_mid.shape[0]
    group_mids = mids // boxes
    tops = list_top.shape[0]
    group_tops = tops // boxes
    vmem = pl.BlockSpec(memory_space=pltpu.VMEM)
    smem = pl.BlockSpec(memory_space=pltpu.SMEM)
    hbm = pl.BlockSpec(memory_space=pl.ANY)
    top_height = 2 * top_width // LANES
    mid_height = 2 * sector // LANES

    chunk = sector * math.gcd(dirs, CHUNK_SECTORS)
    chunks = mid_width // chunk
    outgoing = pl.pallas_call(
        leaf_up,
        in_specs=[hbm, hbm, hbm],
        out_specs=vmem,
        out_shape=jax.ShapeDtypeStruct((dirs, 2 * own_mids, sector), jnp.bfloat16),
        scratch_shapes=[
            pltpu.VMEM((2 * leaves, leaf_width), jnp.bfloat16),
            pltpu.VMEM((octants, mid_width), jnp.float32),
            pltpu.VMEM((chunks, leaf_width, chunk), jnp.bfloat16),
            pltpu.SemaphoreType.DMA((2,)),
            pltpu.SemaphoreType.DMA((chunks,)),
        ],
        compiler_params=params(60),
        cost_estimate=cost(5),
        name="leaf_up",
    )(leaf_out.reshape(2 * leaves, leaf_width), interp_mid, shift_mid)
    mid_own = lax.all_to_all(outgoing, "dir", split_axis=0, concat_axis=0, tiled=True)

    list_width = list_mid.shape[1]
    top_index = [(list_top * (2 * top_height)).reshape(-1), (offset_top * top_height).reshape(-1)]
    own_list = lax.dynamic_slice_in_dim(list_mid, box_index * group_mids, group_mids, 0)
    own_offsets = lax.dynamic_slice_in_dim(offset_mid, box_index * group_mids, group_mids, 0)
    mid_index = [(own_list * (2 * mid_height)).reshape(-1), (own_offsets * mid_height).reshape(-1)]
    rows_top = trans_top.reshape(-1, LANES)
    rows_mid = rows_of(trans_mid)
    table = jax.ShapeDtypeStruct((octants, top_sector), jnp.float32)
    cos_top, sin_top = pl.pallas_call(
        tables,
        in_specs=[vmem],
        out_specs=[vmem] * 2,
        out_shape=[table, table],
        compiler_params=params(16),
        cost_estimate=cost(2),
        name="tables",
    )(shift_top)
    ready = (mid_own, top_index, mid_index, cos_top, sin_top)
    mid_own, top_index, mid_index, cos_top, sin_top = lax.optimization_barrier(ready)

    share = jax.ShapeDtypeStruct((2 * dirs, top_width), jnp.bfloat16)
    top_out = pl.pallas_call(
        top_up,
        in_specs=[vmem] * 4,
        out_specs=[vmem] * boxes,
        out_shape=[share] * boxes,
        compiler_params=params(16),
        cost_estimate=cost(4),
        name="top_up",
    )(mid_own, interp_top, cos_top, sin_top)
    top_all = exchange(top_out)

    groups = {0: follow(mid_own, top_out[0])}
    bits = [1 << k for k in reversed(range(boxes.bit_length() - 1))]
    for bit in bits:
        groups[bit] = swap(groups[0], "box", bit)

    top_in = pl.pallas_call(
        functools.partial(top_translate, list_width),
        in_specs=[hbm, hbm, vmem] + [vmem] * boxes,
        out_specs=[vmem] * boxes,
        out_shape=[share] * boxes,
        scratch_shapes=[
            pltpu.VMEM((rows_top.shape[0] + ROWS, LANES), jnp.float32),
            pltpu.VMEM((2 * (tops + 1) * top_height, LANES), jnp.float32),
            pltpu.VMEM(((tops + 1) * top_height, LANES), jnp.float32),
            pltpu.VMEM(((tops + 1) * top_height, LANES), jnp.float32),
            pltpu.SMEM(top_index[0].shape, jnp.int32),
            pltpu.SMEM(top_index[0].shape, jnp.int32),
            pltpu.SemaphoreType.DMA((4,)),
        ],
        compiler_params=params(16),
        cost_estimate=cost(15),
        name="top_translate",
    )(*top_index, rows_top, *top_all)
    top_back = exchange(top_in)

    for number, bit in enumerate(bits[1:], 1):
        for step in [step for step in groups if step and not step & (2 * bit - 1)]:
            values = follow(groups[step], top_in[0]) if number == 1 else groups[step]
            groups[step ^ bit] = swap(values, "box", bit)

    mid_far = pl.pallas_call(
        functools.partial(mid_translate, list_width),
        in_specs=[hbm, hbm, vmem] + [vmem] * boxes,
        out_specs=vmem,
        out_shape=jax.ShapeDtypeStruct((2, group_mids, sector), jnp.float32),
        scratch_shapes=[
            pltpu.VMEM((2 * (mids + 1) * mid_height, LANES), jnp.float32),
            pltpu.VMEM(((group_mids + 1) * mid_height, LANES), jnp.float32),
            pltpu.VMEM(((group_mids + 1) * mid_height, LANES), jnp.float32),
            pltpu.SMEM(mid_index[0].shape, jnp.int32),
            pltpu.SMEM(mid_index[0].shape, jnp.int32),
            pltpu.SemaphoreType.DMA((4,)),
        ],
        compiler_params=params(16),
        cost_estimate=cost(1),
        name="mid_translate",
    )(*mid_index, rows_mid, *[groups[step] for step in range(boxes)])

    incoming = pl.pallas_call(
        functools.partial(top_down, sector / top_sector),
        in_specs=[vmem] * (4 + boxes),
        out_specs=vmem,
        out_shape=jax.ShapeDtypeStruct((dirs, 2 * own_mids, sector), jnp.bfloat16),
        compiler_params=params(16),
        cost_estimate=cost(1),
        name="top_down",
    )(interp_top, cos_top, sin_top, mid_far, *top_back)
    mid_back = lax.all_to_all(incoming, "dir", split_axis=0, concat_axis=0, tiled=True)

    leaf_in = pl.pallas_call(
        functools.partial(leaf_down, leaf_width / mid_width),
        in_specs=[vmem] * 3,
        out_specs=vmem,
        out_shape=jax.ShapeDtypeStruct((2 * leaves, leaf_width), jnp.float32),
        scratch_shapes=[pltpu.VMEM((leaf_width, 2 * leaves), jnp.float32)],
        compiler_params=params(20),
        cost_estimate=cost(3),
        name="leaf_down",
    )(mid_back, interp_mid, shift_mid)
    return leaf_in.reshape(2, leaves, leaf_width)


def solution(mesh):
    return jax.shard_map(
        on_device,
        mesh=mesh,
        in_specs=(
            P(None, ("box", "dir"), None),
            P(),
            P(),
            P(None, None, "dir"),
            P(),
            P(),
            P("dir", None, None),
            P(None, "dir", None),
            P(None, None, "dir", "box"),
            P(),
            P(),
        ),
        out_specs=P(None, ("box", "dir"), None),
        check_vma=False,
    )
```

```python
import functools
import math

import jax
import jax.numpy as jnp
from jax import lax
from jax.experimental import pallas as pl
from jax.experimental.pallas import tpu as pltpu
from jax.sharding import PartitionSpec as P

SINE = (1.0, -0.16666647791862488, 0.00833289884030819, -0.0001980085507966578, 2.5904087124217767e-06)
COSINE = (1.0, -0.5, 0.04166663438081741, -0.0013888360699638724, 2.476012559782248e-05, -2.6050881274386484e-07)
HEAD_ROWS = 4
UNROLL = 4
LANES = 128
ROWS = 8
AHEAD = 3
DOWN_BLOCKS = 4
CHUNK_SECTORS = 2


def powers(square, factors):
    total = jnp.full_like(square, factors[-1])
    for factor in factors[-2::-1]:
        total = total * square + factor
    return total


def phase(angle):
    half = angle * 0.5
    square = half * half
    sine = half * powers(square, SINE)
    cosine = powers(square, COSINE)
    return 1.0 - 2.0 * sine * sine, 2.0 * sine * cosine


def leaf_up(leaf_hbm, table_hbm, shift_hbm, out_ref, leaf_ref, shift_ref, table_ref, small_sems, table_sems):
    chunks, _, width = table_ref.shape
    octants = shift_ref.shape[0]
    sector = out_ref.shape[2]
    leaf_copy = pltpu.make_async_copy(leaf_hbm, leaf_ref, small_sems.at[0])
    shift_copy = pltpu.make_async_copy(shift_hbm, shift_ref, small_sems.at[1])

    def table_copy(chunk):
        source = table_hbm.at[:, pl.ds(chunk * width, width)]
        return pltpu.make_async_copy(source, table_ref.at[chunk], table_sems.at[chunk])

    leaf_copy.start()
    table_copy(0).start()
    shift_copy.start()
    for chunk in range(1, min(AHEAD, chunks)):
        table_copy(chunk).start()
    leaf_copy.wait()
    shift_copy.wait()
    leaves = leaf_ref.shape[0] // 2
    for chunk in range(chunks):
        table_copy(chunk).wait()
        if chunk + AHEAD < chunks:
            table_copy(chunk + AHEAD).start()
        values = jnp.dot(leaf_ref[...], table_ref[chunk], preferred_element_type=jnp.float32)
        real = values[:leaves].reshape(leaves // octants, octants, width)
        imag = values[leaves:].reshape(leaves // octants, octants, width)
        cos, sin = phase(shift_ref[:, chunk * width : (chunk + 1) * width])
        new_real = jnp.sum(real * cos[None] - imag * sin[None], axis=1)
        new_imag = jnp.sum(real * sin[None] + imag * cos[None], axis=1)
        block = jnp.concatenate([new_real, new_imag], axis=0).astype(out_ref.dtype)
        for part in range(width // sector):
            out_ref[chunk * (width // sector) + part] = block[:, part * sector : (part + 1) * sector]


def spread_rows(block, pattern_ref, first, part):
    pieces = block.shape[1] // LANES
    height = 2 * pieces
    for piece in range(pieces):
        lanes = block[:, piece * LANES : (piece + 1) * LANES]
        start = 2 * first * height + 2 * piece
        pattern_ref[pl.ds(start + part, ROWS, stride=2 * height), :] = lanes
        pattern_ref[pl.ds(start + height + 1 - part, ROWS, stride=2 * height), :] = lanes


def index_copies(hbm_refs, index_refs, sems, head):
    entries = index_refs[0].shape[0]
    parts = (pl.ds(0, head), pl.ds(head, entries - head))
    return [
        [
            pltpu.make_async_copy(hbm_refs[which].at[part], index_refs[which].at[part], sems.at[2 * which + number])
            for which in range(2)
        ]
        for number, part in enumerate(parts)
    ]


def translate(index_refs, first_row, end_row, list_width, trans_ref, pattern_ref, same_ref, cross_ref, height):
    source_ref, offset_ref = index_refs

    def rows_at(step, carry):
        for row in [UNROLL * step + k for k in range(UNROLL)]:
            same = jnp.zeros((height, LANES), jnp.float32)
            cross = jnp.zeros((height, LANES), jnp.float32)
            for entry in range(list_width):
                source = pl.multiple_of(source_ref[row * list_width + entry], height)
                offset = pl.multiple_of(offset_ref[row * list_width + entry], height)
                factor = trans_ref[pl.ds(offset, height), :]
                same += factor * pattern_ref[pl.ds(source, height), :]
                cross += factor * pattern_ref[pl.ds(source + height, height), :]
            place = pl.ds(pl.multiple_of(row * height, height), height)
            same_ref[place, :] = same
            cross_ref[place, :] = cross
        return carry

    lax.fori_loop(first_row // UNROLL, end_row // UNROLL, rows_at, 0)


def gather_rows(same_ref, cross_ref, first, height):
    real, imag = [], []
    for piece in range(height // 2):
        even = pl.ds(first * height + 2 * piece, ROWS, stride=height)
        odd = pl.ds(first * height + 2 * piece + 1, ROWS, stride=height)
        real.append(same_ref[even, :] - same_ref[odd, :])
        imag.append(cross_ref[even, :] + cross_ref[odd, :])
    return jnp.concatenate(real, axis=1), jnp.concatenate(imag, axis=1)


def tables(shift_ref, cos_ref, sin_ref):
    cos_ref[...], sin_ref[...] = phase(shift_ref[:, 0, :])


def place_of(step):
    return lax.axis_index("box") ^ step


def top_up(mid_ref, table_ref, cos_ref, sin_ref, *out_refs):
    tops, double, sector = mid_ref.shape
    octants = cos_ref.shape[0]
    group = mid_ref[...].reshape(tops * double, sector)
    for step, out_ref in enumerate(out_refs):
        width = out_ref.shape[1]
        columns = pl.ds(pl.multiple_of(place_of(step) * width, width), width)
        values = jnp.dot(group, table_ref[0, :, columns], preferred_element_type=jnp.float32)
        values = values.reshape(tops, double, width)
        real, imag = values[:, :octants], values[:, octants:]
        cos, sin = cos_ref[:, columns], sin_ref[:, columns]
        new_real = jnp.sum(real * cos[None] - imag * sin[None], axis=1)
        new_imag = jnp.sum(real * sin[None] + imag * cos[None], axis=1)
        out_ref[...] = jnp.concatenate([new_real, new_imag], axis=0).astype(out_ref.dtype)


def top_translate(list_width, source_hbm, offset_hbm, plane_ref, *rest):
    count = (len(rest) - 7) // 2
    top_refs, out_refs = rest[:count], rest[count : 2 * count]
    trans_ref, pattern_ref, same_ref, cross_ref, *index_refs, sems = rest[2 * count :]
    head = HEAD_ROWS * list_width
    first_copies, later_copies = index_copies((source_hbm, offset_hbm), index_refs, sems, head)
    for copy in first_copies + later_copies:
        copy.start()
    plane = plane_ref.shape[0] // 2
    for part in range(2):
        trans_ref[pl.ds(part, plane, stride=2), :] = plane_ref[part * plane : (part + 1) * plane, :]
    own, width = top_refs[0].shape
    own = own // 2
    height = 2 * width // LANES
    for step, top_ref in enumerate(top_refs):
        rows = top_ref[...].astype(jnp.float32)
        for first in range(0, own, ROWS):
            base = place_of(step) * own + first
            spread_rows(rows[first : first + ROWS], pattern_ref, base, 0)
            spread_rows(rows[own + first : own + first + ROWS], pattern_ref, base, 1)
    for copy in first_copies:
        copy.wait()
    rest = (list_width, trans_ref, pattern_ref, same_ref, cross_ref, height)
    translate(index_refs, 0, HEAD_ROWS, *rest)
    for copy in later_copies:
        copy.wait()
    translate(index_refs, HEAD_ROWS, count * own, *rest)
    for step, out_ref in enumerate(out_refs):
        real, imag = [], []
        for first in range(0, own, ROWS):
            new_real, new_imag = gather_rows(same_ref, cross_ref, place_of(step) * own + first, height)
            real.append(new_real)
            imag.append(new_imag)
        out_ref[...] = jnp.concatenate(real + imag, axis=0).astype(out_ref.dtype)


def mid_translate(list_width, source_hbm, offset_hbm, trans_ref, *rest):
    group_refs = rest[:-7]
    out_ref, pattern_ref, same_ref, cross_ref, *index_refs, sems = rest[-7:]
    head = HEAD_ROWS * list_width
    first_copies, later_copies = index_copies((source_hbm, offset_hbm), index_refs, sems, head)
    for copy in first_copies + later_copies:
        copy.start()
    for step, group_ref in enumerate(group_refs):
        blocks, _, width = group_ref.shape
        height = 2 * width // LANES
        base = place_of(step) * (blocks * ROWS)
        for block in range(blocks):
            rows = group_ref[block].astype(jnp.float32)
            spread_rows(rows[:ROWS], pattern_ref, base + block * ROWS, 0)
            spread_rows(rows[ROWS:], pattern_ref, base + block * ROWS, 1)
    for copy in first_copies:
        copy.wait()
    rest = (list_width, trans_ref, pattern_ref, same_ref, cross_ref, height)
    translate(index_refs, 0, HEAD_ROWS, *rest)
    for copy in later_copies:
        copy.wait()
    translate(index_refs, HEAD_ROWS, out_ref.shape[1], *rest)
    for first in range(0, out_ref.shape[1], ROWS):
        real, imag = gather_rows(same_ref, cross_ref, first, height)
        out_ref[0, first : first + ROWS] = real
        out_ref[1, first : first + ROWS] = imag


def children_of(parents, cos, sin):
    half = parents.shape[0] // 2
    octants, width = cos.shape
    parents = parents.astype(jnp.float32)
    real, imag = parents[:half, None, :], parents[half:, None, :]
    new_real = (real * cos[None] + imag * sin[None]).reshape(half * octants, width)
    new_imag = (imag * cos[None] - real * sin[None]).reshape(half * octants, width)
    return jnp.concatenate([new_real, new_imag], axis=0).astype(jnp.bfloat16)


ADJOINT = (((1,), (1,)), ((), ()))


def top_down(scale, table_ref, cos_ref, sin_ref, far_ref, *rest):
    top_refs, out_ref = rest[:-1], rest[-1]
    total = None
    for step, top_ref in enumerate(top_refs):
        width = top_ref.shape[1]
        columns = pl.ds(pl.multiple_of(place_of(step) * width, width), width)
        children = children_of(top_ref[...], cos_ref[:, columns], sin_ref[:, columns])
        term = lax.dot_general(children, table_ref[0, :, columns], ADJOINT, preferred_element_type=jnp.float32)
        total = term if total is None else total + term
    half = total.shape[0] // 2
    real = far_ref[0] + scale * total[:half]
    imag = far_ref[1] + scale * total[half:]
    owners, rows, _ = out_ref.shape
    rows = rows // 2
    for owner in range(owners):
        place = slice(owner * rows, (owner + 1) * rows)
        out_ref[owner] = jnp.concatenate([real[place], imag[place]], axis=0).astype(out_ref.dtype)


def leaf_down(scale, mid_ref, table_ref, shift_ref, out_hbm, children_ref, total_ref, sems):
    sectors, _, width = mid_ref.shape
    for part in range(sectors):
        columns = slice(part * width, (part + 1) * width)
        cos, sin = phase(shift_ref[:, columns])
        children_ref[:, columns] = children_of(mid_ref[part], cos, sin)
    blocks, _, size = total_ref.shape
    copies = []
    for block in range(blocks):
        place = slice(block * size, (block + 1) * size)
        term = lax.dot_general(table_ref[place, :], children_ref[...], ADJOINT, preferred_element_type=jnp.float32)
        total_ref[block] = term.T * scale
        target = out_hbm.at[:, pl.ds(block * size, size)]
        copies.append(pltpu.make_async_copy(total_ref.at[block], target, sems.at[block]))
        copies[block].start()
    for copy in copies:
        copy.wait()


def cost(microseconds):
    return pl.CostEstimate(flops=int(microseconds * 1.15e9), bytes_accessed=0, transcendentals=0)


def params(mebibytes):
    return pltpu.CompilerParams(vmem_limit_bytes=mebibytes * 1024 * 1024)


def rows_of(trans):
    _, offsets, width = trans.shape
    pieces = width // LANES
    rows = jnp.transpose(trans.reshape(2, offsets, pieces, LANES), (1, 2, 0, 3))
    return rows.reshape(offsets * pieces * 2, LANES)


def swap(values, axis, step):
    size = lax.axis_size(axis)
    return lax.ppermute(values, axis, [(k, k ^ step) for k in range(size)])


def pass_on(values_ref, after_ref, out_ref):
    out_ref[...] = values_ref[...]


def follow(values, after):
    vmem = pl.BlockSpec(memory_space=pltpu.VMEM)
    return pl.pallas_call(
        pass_on,
        in_specs=[vmem, pl.BlockSpec(memory_space=pl.ANY)],
        out_specs=vmem,
        out_shape=jax.ShapeDtypeStruct(values.shape, values.dtype),
        compiler_params=params(16),
        cost_estimate=cost(0.1),
        name="pass_on",
    )(values, after)


def exchange(shares):
    received = list(shares)
    for step in range(1, len(shares)):
        received[step] = swap(shares[step], "box", step)
    return received


def on_device(
    leaf_out,
    interp_mid,
    shift_mid,
    trans_mid,
    list_mid,
    offset_mid,
    interp_top,
    shift_top,
    trans_top,
    list_top,
    offset_top,
):
    boxes = lax.axis_size("box")
    dirs = lax.axis_size("dir")
    box_index = lax.axis_index("box")
    octants = shift_mid.shape[0]
    leaves = leaf_out.shape[1]
    leaf_width, mid_width = interp_mid.shape
    own_mids = leaves // octants
    sector = trans_mid.shape[2]
    top_sector = interp_top.shape[2]
    top_width = trans_top.shape[3]
    mids = list_mid.shape[0]
    group_mids = mids // boxes
    tops = list_top.shape[0]
    group_tops = tops // boxes
    vmem = pl.BlockSpec(memory_space=pltpu.VMEM)
    smem = pl.BlockSpec(memory_space=pltpu.SMEM)
    hbm = pl.BlockSpec(memory_space=pl.ANY)
    top_height = 2 * top_width // LANES
    mid_height = 2 * sector // LANES

    chunk = sector * math.gcd(dirs, CHUNK_SECTORS)
    chunks = mid_width // chunk
    outgoing = pl.pallas_call(
        leaf_up,
        in_specs=[hbm, hbm, hbm],
        out_specs=vmem,
        out_shape=jax.ShapeDtypeStruct((dirs, 2 * own_mids, sector), jnp.bfloat16),
        scratch_shapes=[
            pltpu.VMEM((2 * leaves, leaf_width), jnp.bfloat16),
            pltpu.VMEM((octants, mid_width), jnp.float32),
            pltpu.VMEM((chunks, leaf_width, chunk), jnp.bfloat16),
            pltpu.SemaphoreType.DMA((2,)),
            pltpu.SemaphoreType.DMA((chunks,)),
        ],
        compiler_params=params(60),
        cost_estimate=cost(5),
        name="leaf_up",
    )(leaf_out.reshape(2 * leaves, leaf_width), interp_mid, shift_mid)
    mid_own = lax.all_to_all(outgoing, "dir", split_axis=0, concat_axis=0, tiled=True)

    list_width = list_mid.shape[1]
    top_index = [(list_top * (2 * top_height)).reshape(-1), (offset_top * top_height).reshape(-1)]
    own_list = lax.dynamic_slice_in_dim(list_mid, box_index * group_mids, group_mids, 0)
    own_offsets = lax.dynamic_slice_in_dim(offset_mid, box_index * group_mids, group_mids, 0)
    mid_index = [(own_list * (2 * mid_height)).reshape(-1), (own_offsets * mid_height).reshape(-1)]
    rows_top = trans_top.reshape(-1, LANES)
    rows_mid = rows_of(trans_mid)
    table = jax.ShapeDtypeStruct((octants, top_sector), jnp.float32)
    cos_top, sin_top = pl.pallas_call(
        tables,
        in_specs=[vmem],
        out_specs=[vmem] * 2,
        out_shape=[table, table],
        compiler_params=params(16),
        cost_estimate=cost(2),
        name="tables",
    )(shift_top)
    ready = (mid_own, top_index, mid_index, cos_top, sin_top)
    mid_own, top_index, mid_index, cos_top, sin_top = lax.optimization_barrier(ready)

    share = jax.ShapeDtypeStruct((2 * dirs, top_width), jnp.bfloat16)
    top_out = pl.pallas_call(
        top_up,
        in_specs=[vmem] * 4,
        out_specs=[vmem] * boxes,
        out_shape=[share] * boxes,
        compiler_params=params(16),
        cost_estimate=cost(4),
        name="top_up",
    )(mid_own, interp_top, cos_top, sin_top)
    top_all = exchange(top_out)

    groups = {0: follow(mid_own, top_out[0])}
    bits = [1 << k for k in reversed(range(boxes.bit_length() - 1))]
    for bit in bits:
        groups[bit] = swap(groups[0], "box", bit)

    top_in = pl.pallas_call(
        functools.partial(top_translate, list_width),
        in_specs=[hbm, hbm, vmem] + [vmem] * boxes,
        out_specs=[vmem] * boxes,
        out_shape=[share] * boxes,
        scratch_shapes=[
            pltpu.VMEM((rows_top.shape[0] + ROWS, LANES), jnp.float32),
            pltpu.VMEM((2 * (tops + 1) * top_height, LANES), jnp.float32),
            pltpu.VMEM(((tops + 1) * top_height, LANES), jnp.float32),
            pltpu.VMEM(((tops + 1) * top_height, LANES), jnp.float32),
            pltpu.SMEM(top_index[0].shape, jnp.int32),
            pltpu.SMEM(top_index[0].shape, jnp.int32),
            pltpu.SemaphoreType.DMA((4,)),
        ],
        compiler_params=params(16),
        cost_estimate=cost(15),
        name="top_translate",
    )(*top_index, rows_top, *top_all)
    top_back = exchange(top_in)

    for number, bit in enumerate(bits[1:], 1):
        for step in [step for step in groups if step and not step & (2 * bit - 1)]:
            values = follow(groups[step], top_in[0]) if number == 1 else groups[step]
            groups[step ^ bit] = swap(values, "box", bit)

    mid_far = pl.pallas_call(
        functools.partial(mid_translate, list_width),
        in_specs=[hbm, hbm, vmem] + [vmem] * boxes,
        out_specs=vmem,
        out_shape=jax.ShapeDtypeStruct((2, group_mids, sector), jnp.float32),
        scratch_shapes=[
            pltpu.VMEM((2 * (mids + 1) * mid_height, LANES), jnp.float32),
            pltpu.VMEM(((group_mids + 1) * mid_height, LANES), jnp.float32),
            pltpu.VMEM(((group_mids + 1) * mid_height, LANES), jnp.float32),
            pltpu.SMEM(mid_index[0].shape, jnp.int32),
            pltpu.SMEM(mid_index[0].shape, jnp.int32),
            pltpu.SemaphoreType.DMA((4,)),
        ],
        compiler_params=params(16),
        cost_estimate=cost(1),
        name="mid_translate",
    )(*mid_index, rows_mid, *[groups[step] for step in range(boxes)])

    incoming = pl.pallas_call(
        functools.partial(top_down, sector / top_sector),
        in_specs=[vmem] * (4 + boxes),
        out_specs=vmem,
        out_shape=jax.ShapeDtypeStruct((dirs, 2 * own_mids, sector), jnp.bfloat16),
        compiler_params=params(16),
        cost_estimate=cost(1),
        name="top_down",
    )(interp_top, cos_top, sin_top, mid_far, *top_back)
    mid_back = lax.all_to_all(incoming, "dir", split_axis=0, concat_axis=0, tiled=True)

    leaf_in = pl.pallas_call(
        functools.partial(leaf_down, leaf_width / mid_width),
        in_specs=[vmem] * 3,
        out_specs=hbm,
        out_shape=jax.ShapeDtypeStruct((2 * leaves, leaf_width), jnp.float32),
        scratch_shapes=[
            pltpu.VMEM((2 * leaves, mid_width), jnp.bfloat16),
            pltpu.VMEM((DOWN_BLOCKS, 2 * leaves, leaf_width // DOWN_BLOCKS), jnp.float32),
            pltpu.SemaphoreType.DMA((DOWN_BLOCKS,)),
        ],
        compiler_params=params(20),
        cost_estimate=cost(3),
        name="leaf_down",
    )(mid_back, interp_mid, shift_mid)
    return leaf_in.reshape(2, leaves, leaf_width)


def solution(mesh):
    return jax.shard_map(
        on_device,
        mesh=mesh,
        in_specs=(
            P(None, ("box", "dir"), None),
            P(),
            P(),
            P(None, None, "dir"),
            P(),
            P(),
            P("dir", None, None),
            P(None, "dir", None),
            P(None, None, "dir", "box"),
            P(),
            P(),
        ),
        out_specs=P(None, ("box", "dir"), None),
        check_vma=False,
    )
```
